256 devices in a mesh: ctx: 64 (over x, z, core), head: 4 (over y).
Axes of the slice: x: 4, y: 4, z: 8, core: 2. Of those that a mesh axis runs over, the one named last changes fastest.
Arguments:
- tokens: bfloat16 [65536, 1024], P('ctx'), may hold values from -90 to 90
- w_qkv: bfloat16 [3, 1024, 1024], P(None, None, 'head'), may hold values from -0.1875 to 0.1875
- w_out: bfloat16 [1024, 1024], replicated, may hold values from -0.1875 to 0.1875
- conv_weight: float32 [16, 33], P('head'), may hold values from -0.6 to 0.6
Outputs:
- layer_out: bfloat16 [65536, 1024], P(('ctx', 'head'))
The draws below stay inside these ranges and needn't reach their ends.
All inputs are finite; a program needn't handle non-finite values. Where the reference program divides by a largest or mean magnitude, that divisor is 1e-20 or more.
Results may differ from the reference program's by a relative error of at most 0.017.
The reference program's roundings to bfloat16 on the way (of `kernel_f`, `mid` and `head_out`) count: a program that leaves them out, or rounds other values in their place, can miss the bound.
Values may be sent and summed in bfloat16 or wider, within the bound.
No kernel may reach another device: no remote copies, remote signals or barrier semaphores. Data moves between devices by JAX's collectives and lax.ppermute only.
A program may use at most 192 MiB of HBM per device.

```python
import jax
import jax.numpy as jnp
from jax import lax

H = 16
HD = 64
D = 1024
M = 256
NS_STEPS = 6
KW = 33
TOKENS = 65536


def draw_tokens(key, part):
    key = jax.random.fold_in(key, 11)
    key_off, key_noise = jax.random.split(key, 2)
    seg = TOKENS // M
    segment = jnp.arange(TOKENS) // seg
    offsets = 1.5 * jnp.clip(jax.random.normal(key_off, (M, D), jnp.float32), -4.0, 4.0)
    noise = jnp.clip(jax.random.normal(key_noise, (TOKENS, D), jnp.float32), -4.0, 4.0)
    values = offsets[segment] + noise
    return jnp.clip(values, -90.0, 90.0).astype(jnp.bfloat16)


def level_of(own_key, shape, shards, least, top_value):
    factor_of, own = 1.0, jax.random.fold_in(own_key, 6)
    for axis_at, blocks in shards:
        heights = jnp.exp(jax.random.uniform(jax.random.fold_in(own, axis_at), (blocks,), jnp.float32, least / len(shards), top_value / len(shards)))
        factor_of = factor_of * jnp.repeat(heights, shape[axis_at] // blocks).reshape([-1 if axis == axis_at else 1 for axis in range(len(shape))])
    return factor_of


def bell_draw(own_key, extent, spread, bound, cuts=(), held_as=jnp.bfloat16):
    result = jax.random.normal(own_key, extent, jnp.float32) * spread
    if len(cuts) > 0:
        result = level_of(own_key, extent, cuts, -0.22, 0.18) * result
    return jnp.clip(result, min=-bound, max=bound).astype(held_as)


def setup_inputs(seed: int = 0) -> dict:
    streams_of = jax.random.split(jax.random.key(seed), 5)
    tokens = draw_tokens(jax.random.fold_in(streams_of[4], 71), 0)
    w_qkv = bell_draw(streams_of[1], (3, D, D), D ** -0.5, 0.1875, ((2, 4),))
    w_out = bell_draw(streams_of[2], (D, D), D ** -0.5, 0.1875)
    conv_weight = bell_draw(streams_of[3], (H, KW), 0.1, 0.6, ((0, 4),), jnp.float32)
    return {"tokens": tokens, "w_qkv": w_qkv, "w_out": w_out, "conv_weight": conv_weight}


def softmax_rows(scores):
    top = jnp.max(scores, axis=-1, keepdims=True)
    expo = jnp.exp(scores - top)
    return expo / jnp.sum(expo, axis=-1, keepdims=True)


def newton_pinv(kernel):
    col_sum = jnp.max(jnp.sum(jnp.abs(kernel), axis=0))
    row_sum = jnp.max(jnp.sum(jnp.abs(kernel), axis=1))
    approx = kernel.T / (col_sum * row_sum)
    ident = jnp.eye(kernel.shape[0], dtype=jnp.float32)
    for step in range(NS_STEPS):
        prod = jnp.dot(kernel, approx, precision=lax.Precision.HIGHEST)
        inner = 7.0 * ident - prod
        inner = 15.0 * ident - jnp.dot(prod, inner, precision=lax.Precision.HIGHEST)
        inner = 13.0 * ident - jnp.dot(prod, inner, precision=lax.Precision.HIGHEST)
        approx = 0.25 * jnp.dot(approx, inner, precision=lax.Precision.HIGHEST)
    return approx


def reference(tokens, w_qkv, w_out, conv_weight):
    query = jnp.dot(tokens, w_qkv[0], preferred_element_type=jnp.float32).astype(jnp.bfloat16)
    key = jnp.dot(tokens, w_qkv[1], preferred_element_type=jnp.float32).astype(jnp.bfloat16)
    value = jnp.dot(tokens, w_qkv[2], preferred_element_type=jnp.float32).astype(jnp.bfloat16)
    seg = TOKENS // M
    land_q = jnp.mean(query.astype(jnp.float32).reshape(M, seg, D), axis=1).astype(jnp.bfloat16)
    land_k = jnp.mean(key.astype(jnp.float32).reshape(M, seg, D), axis=1).astype(jnp.bfloat16)
    scale = 1.0 / (HD ** 0.5)
    half = KW // 2
    outputs = []
    for head_id in range(H):
        cols = slice(head_id * HD, (head_id + 1) * HD)
        q_head, k_head, v_head = query[:, cols], key[:, cols], value[:, cols]
        lq_head, lk_head = land_q[:, cols], land_k[:, cols]
        kernel_a = softmax_rows(scale * jnp.dot(lq_head, lk_head.T, preferred_element_type=jnp.float32))
        kernel_f = softmax_rows(scale * jnp.dot(q_head, lk_head.T, preferred_element_type=jnp.float32)).astype(jnp.bfloat16)
        scores_b = scale * jnp.dot(lq_head, k_head.T, preferred_element_type=jnp.float32)
        row_max = jnp.max(scores_b, axis=1, keepdims=True)
        expo = jnp.exp(scores_b - row_max)
        total_b = jnp.sum(expo, axis=1, keepdims=True)
        kernel_bv = jnp.dot(expo.astype(jnp.bfloat16), v_head, preferred_element_type=jnp.float32) / total_b
        pinv_a = newton_pinv(kernel_a)
        mid = jnp.dot(pinv_a, kernel_bv, precision=lax.Precision.HIGHEST).astype(jnp.bfloat16)
        attended = jnp.dot(kernel_f, mid, preferred_element_type=jnp.float32)
        padded = jnp.pad(v_head.astype(jnp.float32), ((half, half), (0, 0)))
        conv = jnp.zeros((TOKENS, HD), jnp.float32)
        for tap in range(KW):
            conv = conv + conv_weight[head_id, tap] * padded[tap:tap + TOKENS]
        outputs.append((attended + conv).astype(jnp.bfloat16))
    head_out = jnp.concatenate(outputs, axis=1)
    return jnp.dot(head_out, w_out, preferred_element_type=jnp.float32).astype(jnp.bfloat16)
```

```python
import jax
import jax.numpy as jnp
from jax import lax
from jax.experimental import pallas as pl
from jax.experimental.pallas import tpu as pltpu
from jax.sharding import PartitionSpec as P

M = 256
NS_STEPS = 6
TAPS = 33
HALF = 16
HEADS = 4
HD = 64
WIDTH = 256
CHIPS = 32
ROWS = 1024
SCALE = 0.125
f32 = jnp.float32
bf16 = jnp.bfloat16
INTERPRET = False
VMEM = pl.BlockSpec(memory_space=pltpu.VMEM)
SMEM = pl.BlockSpec(memory_space=pltpu.SMEM)
HBM = pl.BlockSpec(memory_space=pltpu.HBM)
MIB = 1 << 20


def call(kernel, outs, scratch=(), specs=None, n_in=1, flops=0, moved=0, exps=0, limit=24):
    single = not isinstance(outs, (list, tuple))
    return pl.pallas_call(
        kernel,
        out_shape=outs,
        in_specs=specs or [VMEM] * n_in,
        out_specs=VMEM if single else [VMEM] * len(outs),
        scratch_shapes=list(scratch),
        compiler_params=pltpu.CompilerParams(vmem_limit_bytes=limit * MIB),
        cost_estimate=pl.CostEstimate(flops=flops, bytes_accessed=moved, transcendentals=exps),
        interpret=INTERPRET,
    )


def shaped(shape, dtype):
    return jax.ShapeDtypeStruct(shape, dtype)


def dot_nn(a, b):
    return lax.dot_general(a, b, (((1,), (0,)), ((), ())), preferred_element_type=f32)


def dot_nt(a, b):
    return lax.dot_general(a, b, (((1,), (1,)), ((), ())), preferred_element_type=f32)


def split_2(x):
    high = x.astype(bf16)
    return high, (x - high.astype(f32)).astype(bf16)


def split_3(x):
    high = x.astype(bf16)
    rest = x - high.astype(f32)
    middle = rest.astype(bf16)
    return high, middle, (rest - middle.astype(f32)).astype(bf16)


def dot_wide(a, b, transposed=False):
    (ah, al), (bh, bl) = a, b
    left = jnp.concatenate([ah, ah, al], axis=1)
    if transposed:
        return dot_nt(left, jnp.concatenate([bh, bl, bh], axis=1))
    return dot_nn(left, jnp.concatenate([bh, bl, bh], axis=0))


def head_mask(head):
    lane = lax.broadcasted_iota(jnp.int32, (M, WIDTH), 1)
    return (lane >= head * HD) & (lane < (head + 1) * HD)


def landmarks_kernel(tok_hbm, w_hbm, out_ref, tok_ref, w_ref, rows_ref, sems):
    seg = ROWS // 4
    copies = [
        pltpu.make_async_copy(
            tok_hbm.at[s * seg : (s + 1) * seg, :], tok_ref.at[s * seg : (s + 1) * seg, :], sems.at[s]
        )
        for s in range(4)
    ] + [pltpu.make_async_copy(w_hbm.at[c], w_ref.at[c], sems.at[4 + c]) for c in range(2)]
    for copy in copies:
        copy.start()
    sums = []
    for s in range(4):
        copies[s].wait()
        sums.append(
            jnp.sum(tok_ref[s * seg : (s + 1) * seg, :].astype(f32), axis=0, keepdims=True)
        )
    means = jnp.concatenate(sums, axis=0) * (1.0 / seg)
    high, middle, low = split_3(means)
    stacked = jnp.concatenate(
        [high.astype(f32), middle.astype(f32), low.astype(f32), jnp.zeros_like(means)], axis=0
    ).astype(bf16)
    for kind in range(2):
        copies[4 + kind].wait()
        product = dot_nn(stacked, w_ref[kind])
        land = product[0:4] + product[4:8] + product[8:12]
        for half in range(2):
            rows_ref[pl.ds(2 * kind + half, 4, stride=4), :] = land[:, half * 128 : half * 128 + 128]
    out_ref[...] = jnp.broadcast_to(rows_ref[...].astype(bf16)[None], out_ref.shape)


def project_kernel(
    core_ref, tok_hbm, w_hbm, q_ref, k_ref, vt_ref, near_ref, far_ref, tok_ref, w_ref, sems
):
    seg = ROWS // 4
    copies = [pltpu.make_async_copy(w_hbm.at[c], w_ref.at[c], sems.at[c]) for c in range(3)]
    copies += [
        pltpu.make_async_copy(
            tok_hbm.at[s * seg : (s + 1) * seg, :], tok_ref.at[s * seg : (s + 1) * seg, :], sems.at[3 + s]
        )
        for s in range(4)
    ]
    for copy in copies:
        copy.start()
    for copy in copies[:3]:
        copy.wait()
    edges = []
    for s in range(4):
        copies[3 + s].wait()
        rows = slice(s * seg, (s + 1) * seg)
        tok = tok_ref[rows, :]
        q_ref[rows, :] = dot_nn(tok, w_ref[0]).astype(bf16)
        k_ref[rows, :] = dot_nn(tok, w_ref[1]).astype(bf16)
        value = dot_nn(tok, w_ref[2]).astype(bf16)
        vt_ref[:, rows] = value.T
        edges.append(value)
    first = edges[0][:HALF].astype(f32)
    last = edges[3][seg - HALF :].astype(f32)
    is_first = core_ref[0] == 0
    near_ref[...] = jnp.where(is_first, last, first).astype(bf16)
    far_ref[...] = jnp.where(is_first, first, last).astype(bf16)


def scores_kernel(
    core_ref, own_ref, other_ref, k_ref, vt_ref, lq_ref, lk_ref, keep_ref, send_ref, land_rows, acc, level
):
    core = core_ref[0]
    count = CHIPS * 16
    land_rows[pl.ds(core * count, count), :] = own_ref[...].astype(f32).reshape(count, 128)
    land_rows[pl.ds((1 - core) * count, count), :] = other_ref[...].astype(f32).reshape(count, 128)
    picked = [land_rows[pl.ds(j, M, stride=4), :] for j in range(4)]
    lq = jnp.concatenate(picked[:2], axis=1)
    lk = jnp.concatenate(picked[2:], axis=1)
    lq_ref[...] = lq.astype(bf16)
    lk_ref[...] = lk.astype(bf16)
    key = k_ref[...]
    level[...] = jnp.zeros(level.shape, f32)
    for head in range(HEADS):
        rows = slice(head * HD, (head + 1) * HD)
        own = jnp.where(head_mask(head), lq, 0.0).astype(bf16)
        scores = dot_nt(key, own)
        top = jnp.max(scores, axis=0, keepdims=True)
        expo = jnp.exp((scores - top) * SCALE)
        total = jnp.sum(expo, axis=0, keepdims=True)
        acc[rows, :] = dot_nn(vt_ref[rows, :], expo.astype(bf16)) / total
        at = 8 * (head // 2) + head % 2
        level[at : at + 1, :] = top * SCALE + jnp.log(total)
    for ref, side in ((keep_ref, core), (send_ref, 1 - core)):
        ref[0:128, :] = acc[pl.ds(pl.multiple_of(side * 128, 128), 128), :]
        ref[128:136, :] = level[pl.ds(pl.multiple_of(side * 8, 8), 8), :]


def combine_kernel(keep_ref, other_ref, out_ref, acc_low, acc_high, out_rows):
    acc_rows = (acc_low, acc_high)
    span = CHIPS // 2 * 16
    for head in range(2):
        rows = slice(head * HD, (head + 1) * HD)
        level_a = keep_ref[128 + head : 129 + head, :]
        level_b = other_ref[128 + head : 129 + head, :]
        top = jnp.maximum(level_a, level_b)
        weight_a = jnp.exp(level_a - top)
        weight_b = jnp.exp(level_b - top)
        total = weight_a + weight_b
        mean = keep_ref[rows, :] * (weight_a / total) + other_ref[rows, :] * (weight_b / total)
        pieces = split_3(top + jnp.log(total))
        for half in range(2):
            lanes = slice(half * 128, half * 128 + 128)
            acc_rows[half][rows, :] = mean[:, lanes]
            for c in range(3):
                out_rows[pl.ds(head * span + half * 8 + 4 + c, 16, stride=16), :] = jnp.broadcast_to(
                    pieces[c][:, lanes].astype(f32), (16, 128)
                )
            out_rows[pl.ds(head * span + half * 8 + 7, 16, stride=16), :] = jnp.zeros((16, 128), f32)
    for half in range(2):
        for r in range(4):
            out_rows[pl.ds(half * 8 + r, CHIPS, stride=16), :] = acc_rows[half][
                pl.ds(r, CHIPS, stride=4), :
            ]
    out_ref[...] = out_rows[...].reshape(CHIPS, 16, 128).astype(bf16)


def pinv_kernel(head_ref, lq_ref, lk_ref, w_ref):
    own = jnp.where(head_mask(head_ref[0]), lq_ref[...].astype(f32), 0.0).astype(bf16)
    scores = dot_nt(own, lk_ref[...]) * SCALE
    expo = jnp.exp(scores - jnp.max(scores, axis=1, keepdims=True))
    kernel = expo / jnp.sum(expo, axis=1, keepdims=True)
    col_sum = jnp.max(jnp.sum(kernel, axis=0, keepdims=True))
    row_sum = jnp.max(jnp.sum(kernel, axis=1, keepdims=True))
    approx = kernel / (col_sum * row_sum)
    diagonal = lax.broadcasted_iota(jnp.int32, (M, M), 0) == lax.broadcasted_iota(jnp.int32, (M, M), 1)
    ident = jnp.where(diagonal, 1.0, 0.0)
    prod = dot_wide(split_2(approx), split_2(kernel), transposed=True)
    for step in range(NS_STEPS):
        parts = split_2(prod)
        square = dot_wide(parts, parts)
        last = step == NS_STEPS - 1
        right = 7.0 * ident - prod
        if not last:
            right = jnp.concatenate([right, 7.0 * prod - square], axis=1)
        both = dot_wide(split_2(square), split_2(right))
        factor = 0.25 * (13.0 * ident - 15.0 * prod + both[:, :M])
        if not last:
            prod = 0.25 * (13.0 * prod - 15.0 * square + both[:, M:])
        approx = dot_wide(split_2(factor), split_2(approx))
    w_ref[...] = approx


def middle_kernel(parts_ref, w_ref, out_ref, part_rows, out_rows):
    part_rows[...] = parts_ref[...].astype(f32).reshape(CHIPS * 16, 128)
    halves = []
    for half in range(2):
        rows = [part_rows[pl.ds(half * 8 + r, CHIPS, stride=16), :] for r in range(7)]
        level = (rows[4] + rows[5]) + rows[6]
        weight = jnp.exp(level - jnp.max(level, axis=0, keepdims=True))
        weight = weight / jnp.sum(weight, axis=0, keepdims=True)
        halves.append(
            jnp.concatenate(
                [jnp.sum(weight * rows[r], axis=0, keepdims=True) for r in range(4)]
                + [jnp.zeros((4, 128), f32)],
                axis=0,
            )
        )
    bv = jnp.concatenate(halves, axis=1)
    mid = dot_wide(split_2(bv), split_2(w_ref[...]))[0:4]
    for half in range(2):
        out_rows[pl.ds(half, 4, stride=2), :] = mid[:, half * 128 : half * 128 + 128]
    out_ref[...] = jnp.broadcast_to(out_rows[...].astype(bf16)[None], out_ref.shape)


def token_kernel(lk_ref, q_ref, out_ref):
    query = q_ref[...]
    lk = lk_ref[...].astype(f32)
    for head in range(HEADS):
        own = jnp.where(head_mask(head), lk, 0.0).astype(bf16)
        scores = dot_nt(own, query)
        expo = jnp.exp((scores - jnp.max(scores, axis=0, keepdims=True)) * SCALE)
        out_ref[head] = (expo / jnp.sum(expo, axis=0, keepdims=True)).astype(bf16)


def conv_kernel(core_ref, vt_ref, near_ref, far_ref, cw_ref, out_ref):
    blocks = ROWS // 128
    is_first = core_ref[0] == 0
    near = near_ref[...].astype(f32)
    far = far_ref[...].astype(f32)
    empty = jnp.zeros((128 - HALF, WIDTH), f32)
    before = jnp.concatenate([empty, jnp.where(is_first, far, near)], axis=0).T.astype(bf16)
    after = jnp.concatenate([jnp.where(is_first, near, far), empty], axis=0).T.astype(bf16)
    for head in range(HEADS):
        taps = jnp.concatenate([cw_ref[head : head + 1, :], jnp.zeros((1, 384 - TAPS), f32)], axis=1)
        band = pltpu.roll(
            jnp.broadcast_to(taps, (128, 384)), 128 - HALF, 1, stride=1, stride_axis=0
        )
        high, low = split_2(band)
        rows = slice(head * HD, (head + 1) * HD)
        pieces = [before[rows, :]]
        pieces += [vt_ref[rows, b * 128 : b * 128 + 128] for b in range(blocks)]
        pieces += [after[rows, :]]
        windows = jnp.concatenate(
            [jnp.concatenate(pieces[b : b + 3] * 2, axis=1) for b in range(blocks)], axis=0
        )
        out = dot_nt(windows, jnp.concatenate([high, low], axis=1))
        for b in range(blocks):
            out_ref[rows, b * 128 : b * 128 + 128] = out[b * HD : (b + 1) * HD, :]


def attend_kernel(core_ref, own_ref, other_ref, kf_ref, conv_ref, out_ref, mid_rows):
    core = core_ref[0]
    count = CHIPS * 8
    mid_rows[pl.ds(core * count, count), :] = own_ref[...].astype(f32).reshape(count, 128)
    mid_rows[pl.ds((1 - core) * count, count), :] = other_ref[...].astype(f32).reshape(count, 128)
    mid = jnp.concatenate(
        [mid_rows[pl.ds(half, M, stride=2), :] for half in range(2)], axis=1
    ).astype(bf16)
    outs = []
    for head in range(HEADS):
        rows = slice(head * HD, (head + 1) * HD)
        outs.append((dot_nn(mid[rows, :], kf_ref[head]) + conv_ref[rows, :]).astype(bf16))
    out = jnp.concatenate(outs, axis=0).T
    out_ref[...] = out.reshape(out_ref.shape)


def output_kernel(x_ref, w_ref, out_ref):
    groups = x_ref.shape[0]
    joined = jnp.concatenate([x_ref[g] for g in range(groups)], axis=1)
    out_ref[...] = dot_nn(joined, w_ref[...]).astype(bf16)


def body(tokens, w_qkv, w_out, conv_weight):
    groups = lax.axis_size("head")
    same_core = [[2 * chip + core for chip in range(CHIPS)] for core in range(2)]
    swap = [(i, i ^ 1) for i in range(2 * CHIPS)]
    onward = [(2 * chip + 1, 2 * chip + 2) for chip in range(CHIPS - 1)]
    onward += [(b, a) for a, b in onward]
    place = lax.axis_index("ctx").astype(jnp.int32)
    core = (place % 2).reshape(1)
    head_id = (2 * (place % 2) + place // CHIPS).reshape(1)

    def exchange(x):
        return lax.all_to_all(x, "ctx", 0, 0, tiled=True, axis_index_groups=same_core)

    own = call(
        landmarks_kernel,
        shaped((CHIPS, 16, 128), bf16),
        [
            pltpu.VMEM((ROWS, 1024), bf16),
            pltpu.VMEM((2, 1024, WIDTH), bf16),
            pltpu.VMEM((16, 128), f32),
            pltpu.SemaphoreType.DMA((6,)),
        ],
        specs=[HBM, HBM],
        flops=2 * 16 * 1024 * 512,
        moved=3 * MIB,
    )(tokens, w_qkv)
    land = exchange(own)
    land_other = lax.ppermute(land, "ctx", swap)
    query, key, value_t, near, far = call(
        project_kernel,
        [
            shaped((ROWS, WIDTH), bf16),
            shaped((ROWS, WIDTH), bf16),
            shaped((WIDTH, ROWS), bf16),
            shaped((HALF, WIDTH), bf16),
            shaped((HALF, WIDTH), bf16),
        ],
        [
            pltpu.VMEM((ROWS, 1024), bf16),
            pltpu.VMEM((3, 1024, WIDTH), bf16),
            pltpu.SemaphoreType.DMA((7,)),
        ],
        specs=[SMEM, HBM, HBM],
        flops=2 * 1024 * 1024 * 768,
        moved=6 * MIB,
    )(core, tokens, w_qkv)
    near = lax.ppermute(near, "ctx", swap)
    far = lax.ppermute(far, "ctx", onward)
    land_q, land_k, keep, send = call(
        scores_kernel,
        [
            shaped((M, WIDTH), bf16),
            shaped((M, WIDTH), bf16),
            shaped((136, M), f32),
            shaped((136, M), f32),
        ],
        [pltpu.VMEM((CHIPS * 32, 128), f32), pltpu.VMEM((M, M), f32), pltpu.VMEM((16, M), f32)],
        specs=[SMEM] + [VMEM] * 4,
        flops=4 * 4 * 1024 * 256 * 256,
        moved=2 * MIB,
        exps=MIB,
    )(core, land, land_other, key, value_t)
    received = lax.ppermute(send, "ctx", swap)
    parts = call(
        combine_kernel,
        shaped((CHIPS, 16, 128), bf16),
        [pltpu.VMEM((128, 128), f32), pltpu.VMEM((128, 128), f32), pltpu.VMEM((CHIPS * 16, 128), f32)],
        n_in=2,
        flops=MIB,
        moved=MIB // 2,
    )(keep, received)
    gathered = exchange(parts)
    inverse = call(
        pinv_kernel,
        shaped((M, M), f32),
        specs=[SMEM, VMEM, VMEM],
        flops=24 * 3 * 2 * 256**3,
        moved=MIB // 2,
        exps=65536,
    )(head_id, land_q, land_k)
    mid_own = call(
        middle_kernel,
        shaped((CHIPS, 8, 128), bf16),
        [pltpu.VMEM((CHIPS * 16, 128), f32), pltpu.VMEM((8, 128), f32)],
        n_in=2,
        flops=6 * 8 * 256 * 256,
        moved=MIB // 2,
    )(gathered, inverse)
    mids = exchange(mid_own)
    mids_other = lax.ppermute(mids, "ctx", swap)
    kernel_f = call(
        token_kernel,
        shaped((HEADS, M, ROWS), bf16),
        n_in=2,
        flops=4 * 2 * 1024 * 256 * 256,
        moved=3 * MIB,
        exps=MIB,
    )(land_k, query)
    conv = call(
        conv_kernel,
        shaped((WIDTH, ROWS), f32),
        specs=[SMEM] + [VMEM] * 4,
        flops=2 * 512 * 768 * 512,
        moved=2 * MIB,
    )(core, value_t, near, far, conv_weight)
    head_out = call(
        attend_kernel,
        shaped((groups, ROWS // groups, WIDTH), bf16),
        [pltpu.VMEM((CHIPS * 16, 128), f32)],
        specs=[SMEM] + [VMEM] * 4,
        flops=4 * 2 * 64 * 256 * 1024,
        moved=4 * MIB,
    )(core, mids, mids_other, kernel_f, conv)
    regrouped = lax.all_to_all(head_out, "head", 0, 0, tiled=True)
    return call(
        output_kernel,
        shaped((ROWS // groups, w_out.shape[1]), bf16),
        n_in=2,
        flops=2 * 256 * 1024 * 1024,
        moved=3 * MIB,
    )(regrouped, w_out)


def solution(mesh):
    placed = (P("ctx", None), P(None, None, "head"), P(), P("head", None))
    return jax.shard_map(
        body, mesh=mesh, in_specs=placed, out_specs=P(("ctx", "head"), None), check_vma=False
    )
```

```python
import jax
import jax.numpy as jnp
from jax import lax
from jax.experimental import pallas as pl
from jax.experimental.pallas import tpu as pltpu
from jax.sharding import PartitionSpec as P

M = 256
NS_STEPS = 6
TAPS = 33
HALF = 16
HEADS = 4
HD = 64
WIDTH = 256
CHIPS = 32
ROWS = 1024
SCALE = 0.125
f32 = jnp.float32
bf16 = jnp.bfloat16
INTERPRET = False
VMEM = pl.BlockSpec(memory_space=pltpu.VMEM)
SMEM = pl.BlockSpec(memory_space=pltpu.SMEM)
HBM = pl.BlockSpec(memory_space=pltpu.HBM)
MIB = 1 << 20


def call(
    kernel, outs, scratch=(), specs=None, out_specs=None, n_in=1, flops=0, moved=0, exps=0, limit=24
):
    single = not isinstance(outs, (list, tuple))
    return pl.pallas_call(
        kernel,
        out_shape=outs,
        in_specs=specs or [VMEM] * n_in,
        out_specs=out_specs or (VMEM if single else [VMEM] * len(outs)),
        scratch_shapes=list(scratch),
        compiler_params=pltpu.CompilerParams(vmem_limit_bytes=limit * MIB),
        cost_estimate=pl.CostEstimate(flops=flops, bytes_accessed=moved, transcendentals=exps),
        interpret=INTERPRET,
    )


def shaped(shape, dtype):
    return jax.ShapeDtypeStruct(shape, dtype)


def dot_nn(a, b):
    return lax.dot_general(a, b, (((1,), (0,)), ((), ())), preferred_element_type=f32)


def dot_nt(a, b):
    return lax.dot_general(a, b, (((1,), (1,)), ((), ())), preferred_element_type=f32)


def split_2(x):
    high = x.astype(bf16)
    return high, (x - high.astype(f32)).astype(bf16)


def split_3(x):
    high = x.astype(bf16)
    rest = x - high.astype(f32)
    middle = rest.astype(bf16)
    return high, middle, (rest - middle.astype(f32)).astype(bf16)


def dot_wide(a, b, transposed=False):
    (ah, al), (bh, bl) = a, b
    left = jnp.concatenate([ah, ah, al], axis=1)
    if transposed:
        return dot_nt(left, jnp.concatenate([bh, bl, bh], axis=1))
    return dot_nn(left, jnp.concatenate([bh, bl, bh], axis=0))


def head_mask(head):
    lane = lax.broadcasted_iota(jnp.int32, (M, WIDTH), 1)
    return (lane >= head * HD) & (lane < (head + 1) * HD)


def landmarks_kernel(tok_hbm, w_hbm, out_ref, tok_ref, w_ref, rows_ref, sems):
    seg = ROWS // 4
    copies = [
        pltpu.make_async_copy(
            tok_hbm.at[s * seg : (s + 1) * seg, :], tok_ref.at[s * seg : (s + 1) * seg, :], sems.at[s]
        )
        for s in range(4)
    ] + [pltpu.make_async_copy(w_hbm.at[c], w_ref.at[c], sems.at[4 + c]) for c in range(2)]
    for copy in copies:
        copy.start()
    sums = []
    for s in range(4):
        copies[s].wait()
        sums.append(
            jnp.sum(tok_ref[s * seg : (s + 1) * seg, :].astype(f32), axis=0, keepdims=True)
        )
    means = jnp.concatenate(sums, axis=0) * (1.0 / seg)
    high, middle, low = split_3(means)
    stacked = jnp.concatenate(
        [high.astype(f32), middle.astype(f32), low.astype(f32), jnp.zeros_like(means)], axis=0
    ).astype(bf16)
    for kind in range(2):
        copies[4 + kind].wait()
        product = dot_nn(stacked, w_ref[kind])
        land = product[0:4] + product[4:8] + product[8:12]
        for half in range(2):
            rows_ref[pl.ds(2 * kind + half, 4, stride=4), :] = land[:, half * 128 : half * 128 + 128]
    out_ref[...] = jnp.broadcast_to(rows_ref[...].astype(bf16)[None], out_ref.shape)


def project_kernel(
    core_ref, tok_hbm, w_hbm, q_ref, k_ref, vt_ref, near_ref, far_ref, tok_ref, w_ref, sems
):
    seg = ROWS // 4
    copies = [pltpu.make_async_copy(w_hbm.at[c], w_ref.at[c], sems.at[c]) for c in range(3)]
    copies += [
        pltpu.make_async_copy(
            tok_hbm.at[s * seg : (s + 1) * seg, :], tok_ref.at[s * seg : (s + 1) * seg, :], sems.at[3 + s]
        )
        for s in range(4)
    ]
    for copy in copies:
        copy.start()
    for copy in copies[:3]:
        copy.wait()
    edges = []
    for s in range(4):
        copies[3 + s].wait()
        rows = slice(s * seg, (s + 1) * seg)
        tok = tok_ref[rows, :]
        q_ref[rows, :] = dot_nn(tok, w_ref[0]).astype(bf16)
        k_ref[rows, :] = dot_nn(tok, w_ref[1]).astype(bf16)
        value = dot_nn(tok, w_ref[2]).astype(bf16)
        vt_ref[:, rows] = value.T
        edges.append(value)
    first = edges[0][:HALF].astype(f32)
    last = edges[3][seg - HALF :].astype(f32)
    is_first = core_ref[0] == 0
    near_ref[...] = jnp.where(is_first, last, first).astype(bf16)
    far_ref[...] = jnp.where(is_first, first, last).astype(bf16)


def scores_kernel(
    core_ref,
    own_ref,
    other_ref,
    k_hbm,
    vt_hbm,
    lq_ref,
    lk_ref,
    keep_ref,
    send_ref,
    k_ref,
    vt_ref,
    land_rows,
    acc,
    level,
    sems,
):
    loads = [
        pltpu.make_async_copy(k_hbm, k_ref, sems.at[0]),
        pltpu.make_async_copy(vt_hbm, vt_ref, sems.at[1]),
    ]
    for copy in loads:
        copy.start()
    core = core_ref[0]
    count = CHIPS * 16
    land_rows[pl.ds(core * count, count), :] = own_ref[...].astype(f32).reshape(count, 128)
    land_rows[pl.ds((1 - core) * count, count), :] = other_ref[...].astype(f32).reshape(count, 128)
    picked = [land_rows[pl.ds(j, M, stride=4), :] for j in range(4)]
    lq = jnp.concatenate(picked[:2], axis=1)
    lk = jnp.concatenate(picked[2:], axis=1)
    lq_ref[...] = lq.astype(bf16)
    lk_ref[...] = lk.astype(bf16)
    level[...] = jnp.zeros(level.shape, f32)
    loads[0].wait()
    for head in range(HEADS):
        rows = slice(head * HD, (head + 1) * HD)
        own = jnp.where(head_mask(head), lq, 0.0).astype(bf16)
        scores = dot_nt(k_ref[...], own)
        top = jnp.max(scores, axis=0, keepdims=True)
        expo = jnp.exp((scores - top) * SCALE)
        total = jnp.sum(expo, axis=0, keepdims=True)
        if head == 0:
            loads[1].wait()
        acc[rows, :] = dot_nn(vt_ref[rows, :], expo.astype(bf16)) / total
        at = 8 * (head // 2) + head % 2
        level[at : at + 1, :] = top * SCALE + jnp.log(total)
    for ref, side in ((keep_ref, core), (send_ref, 1 - core)):
        ref[0:128, :] = acc[pl.ds(pl.multiple_of(side * 128, 128), 128), :]
        ref[128:136, :] = level[pl.ds(pl.multiple_of(side * 8, 8), 8), :]


def combine_kernel(keep_ref, other_ref, out_ref, acc_low, acc_high, out_rows):
    acc_rows = (acc_low, acc_high)
    span = CHIPS // 2 * 16
    for head in range(2):
        rows = slice(head * HD, (head + 1) * HD)
        level_a = keep_ref[128 + head : 129 + head, :]
        level_b = other_ref[128 + head : 129 + head, :]
        top = jnp.maximum(level_a, level_b)
        weight_a = jnp.exp(level_a - top)
        weight_b = jnp.exp(level_b - top)
        total = weight_a + weight_b
        mean = keep_ref[rows, :] * (weight_a / total) + other_ref[rows, :] * (weight_b / total)
        pieces = split_3(top + jnp.log(total))
        for half in range(2):
            lanes = slice(half * 128, half * 128 + 128)
            acc_rows[half][rows, :] = mean[:, lanes]
            for c in range(3):
                out_rows[pl.ds(head * span + half * 8 + 4 + c, 16, stride=16), :] = jnp.broadcast_to(
                    pieces[c][:, lanes].astype(f32), (16, 128)
                )
            out_rows[pl.ds(head * span + half * 8 + 7, 16, stride=16), :] = jnp.zeros((16, 128), f32)
    for half in range(2):
        for r in range(4):
            out_rows[pl.ds(half * 8 + r, CHIPS, stride=16), :] = acc_rows[half][
                pl.ds(r, CHIPS, stride=4), :
            ]
    out_ref[...] = out_rows[...].reshape(CHIPS, 16, 128).astype(bf16)


def pinv_kernel(head_ref, lq_ref, lk_ref, w_ref):
    own = jnp.where(head_mask(head_ref[0]), lq_ref[...].astype(f32), 0.0).astype(bf16)
    scores = dot_nt(own, lk_ref[...]) * SCALE
    expo = jnp.exp(scores - jnp.max(scores, axis=1, keepdims=True))
    kernel = expo / jnp.sum(expo, axis=1, keepdims=True)
    col_sum = jnp.max(jnp.sum(kernel, axis=0, keepdims=True))
    row_sum = jnp.max(jnp.sum(kernel, axis=1, keepdims=True))
    approx = kernel / (col_sum * row_sum)
    diagonal = lax.broadcasted_iota(jnp.int32, (M, M), 0) == lax.broadcasted_iota(jnp.int32, (M, M), 1)
    ident = jnp.where(diagonal, 1.0, 0.0)
    prod = dot_wide(split_2(approx), split_2(kernel), transposed=True)
    for step in range(NS_STEPS):
        parts = split_2(prod)
        square = dot_wide(parts, parts)
        last = step == NS_STEPS - 1
        right = 7.0 * ident - prod
        if not last:
            right = jnp.concatenate([right, 7.0 * prod - square], axis=1)
        both = dot_wide(split_2(square), split_2(right))
        factor = 0.25 * (13.0 * ident - 15.0 * prod + both[:, :M])
        if not last:
            prod = 0.25 * (13.0 * prod - 15.0 * square + both[:, M:])
        approx = dot_wide(split_2(factor), split_2(approx))
    w_ref[...] = approx


def middle_kernel(parts_ref, w_ref, out_ref, part_rows, out_rows):
    part_rows[...] = parts_ref[...].astype(f32).reshape(CHIPS * 16, 128)
    halves = []
    for half in range(2):
        rows = [part_rows[pl.ds(half * 8 + r, CHIPS, stride=16), :] for r in range(7)]
        level = (rows[4] + rows[5]) + rows[6]
        weight = jnp.exp(level - jnp.max(level, axis=0, keepdims=True))
        weight = weight / jnp.sum(weight, axis=0, keepdims=True)
        halves.append(
            jnp.concatenate(
                [jnp.sum(weight * rows[r], axis=0, keepdims=True) for r in range(4)]
                + [jnp.zeros((4, 128), f32)],
                axis=0,
            )
        )
    bv = jnp.concatenate(halves, axis=1)
    mid = dot_wide(split_2(bv), split_2(w_ref[...]))[0:4]
    for half in range(2):
        out_rows[pl.ds(half, 4, stride=2), :] = mid[:, half * 128 : half * 128 + 128]
    out_ref[...] = jnp.broadcast_to(out_rows[...].astype(bf16)[None], out_ref.shape)


def token_kernel(lk_ref, q_ref, out_ref):
    query = q_ref[...]
    lk = lk_ref[...].astype(f32)
    for head in range(HEADS):
        own = jnp.where(head_mask(head), lk, 0.0).astype(bf16)
        scores = dot_nt(own, query)
        expo = jnp.exp((scores - jnp.max(scores, axis=0, keepdims=True)) * SCALE)
        out_ref[head] = (expo / jnp.sum(expo, axis=0, keepdims=True)).astype(bf16)


def conv_kernel(core_ref, vt_ref, near_ref, far_ref, cw_ref, out_ref):
    blocks = ROWS // 128
    is_first = core_ref[0] == 0
    near = near_ref[...].astype(f32)
    far = far_ref[...].astype(f32)
    empty = jnp.zeros((128 - HALF, WIDTH), f32)
    before = jnp.concatenate([empty, jnp.where(is_first, far, near)], axis=0).T.astype(bf16)
    after = jnp.concatenate([jnp.where(is_first, near, far), empty], axis=0).T.astype(bf16)
    for head in range(HEADS):
        taps = jnp.concatenate([cw_ref[head : head + 1, :], jnp.zeros((1, 384 - TAPS), f32)], axis=1)
        band = pltpu.roll(
            jnp.broadcast_to(taps, (128, 384)), 128 - HALF, 1, stride=1, stride_axis=0
        )
        high, low = split_2(band)
        rows = slice(head * HD, (head + 1) * HD)
        pieces = [before[rows, :]]
        pieces += [vt_ref[rows, b * 128 : b * 128 + 128] for b in range(blocks)]
        pieces += [after[rows, :]]
        windows = jnp.concatenate(
            [jnp.concatenate(pieces[b : b + 3] * 2, axis=1) for b in range(blocks)], axis=0
        )
        out = dot_nt(windows, jnp.concatenate([high, low], axis=1))
        for b in range(blocks):
            out_ref[rows, b * 128 : b * 128 + 128] = out[b * HD : (b + 1) * HD, :]


def attend_kernel(core_ref, group_ref, own_ref, other_ref, kf_ref, conv_ref, *refs):
    out_refs, (mid_rows, joined) = refs[:-2], refs[-2:]
    groups = len(out_refs)
    seg = ROWS // groups
    core = core_ref[0]
    count = CHIPS * 8
    mid_rows[pl.ds(core * count, count), :] = own_ref[...].astype(f32).reshape(count, 128)
    mid_rows[pl.ds((1 - core) * count, count), :] = other_ref[...].astype(f32).reshape(count, 128)
    mid = jnp.concatenate(
        [mid_rows[pl.ds(half, M, stride=2), :] for half in range(2)], axis=1
    ).astype(bf16)
    outs = []
    for head in range(HEADS):
        rows = slice(head * HD, (head + 1) * HD)
        outs.append((dot_nn(mid[rows, :], kf_ref[head]) + conv_ref[rows, :]).astype(bf16))
    joined[...] = jnp.concatenate(outs, axis=0).T
    for step in range(groups):
        to = lax.rem(group_ref[0] + step, groups)
        out_refs[step][...] = joined[pl.ds(pl.multiple_of(to * seg, seg), seg), :]


def output_kernel(group_ref, w_ref, *refs):
    x_refs, out_ref = refs[:-1], refs[-1]
    groups = len(x_refs)
    total = None
    for step in range(groups):
        source = lax.rem(group_ref[0] + groups - step, groups)
        rows = pl.ds(pl.multiple_of(source * WIDTH, WIDTH), WIDTH)
        part = dot_nn(x_refs[step][...], w_ref[rows, :])
        total = part if total is None else total + part
    out_ref[...] = total.astype(bf16)


def body(tokens, w_qkv, w_out, conv_weight):
    groups = lax.axis_size("head")
    same_core = [[2 * chip + core for chip in range(CHIPS)] for core in range(2)]
    swap = [(i, i ^ 1) for i in range(2 * CHIPS)]
    onward = [(2 * chip + 1, 2 * chip + 2) for chip in range(CHIPS - 1)]
    onward += [(b, a) for a, b in onward]
    place = lax.axis_index("ctx").astype(jnp.int32)
    group = lax.axis_index("head").astype(jnp.int32).reshape(1)
    seg = ROWS // groups
    core = (place % 2).reshape(1)
    head_id = (2 * (place % 2) + place // CHIPS).reshape(1)

    def exchange(x):
        return lax.all_to_all(x, "ctx", 0, 0, tiled=True, axis_index_groups=same_core)

    own = call(
        landmarks_kernel,
        shaped((CHIPS, 16, 128), bf16),
        [
            pltpu.VMEM((ROWS, 1024), bf16),
            pltpu.VMEM((2, 1024, WIDTH), bf16),
            pltpu.VMEM((16, 128), f32),
            pltpu.SemaphoreType.DMA((6,)),
        ],
        specs=[HBM, HBM],
        flops=2 * 16 * 1024 * 512,
        moved=3 * MIB,
        limit=63,
    )(tokens, w_qkv)
    land = exchange(own)
    query, key, value_t, near, far = call(
        project_kernel,
        [
            shaped((ROWS, WIDTH), bf16),
            shaped((ROWS, WIDTH), bf16),
            shaped((WIDTH, ROWS), bf16),
            shaped((HALF, WIDTH), bf16),
            shaped((HALF, WIDTH), bf16),
        ],
        [
            pltpu.VMEM((ROWS, 1024), bf16),
            pltpu.VMEM((3, 1024, WIDTH), bf16),
            pltpu.SemaphoreType.DMA((7,)),
        ],
        specs=[SMEM, HBM, HBM],
        flops=2 * 1024 * 1024 * 768,
        moved=6 * MIB,
        limit=48,
    )(core, tokens, w_qkv)
    land, query, key, value_t, near, far = lax.optimization_barrier(
        (land, query, key, value_t, near, far)
    )
    land_other = lax.ppermute(land, "ctx", swap)
    near = lax.ppermute(near, "ctx", swap)
    far = lax.ppermute(far, "ctx", onward)
    land_q, land_k, keep, send = call(
        scores_kernel,
        [
            shaped((M, WIDTH), bf16),
            shaped((M, WIDTH), bf16),
            shaped((136, M), f32),
            shaped((136, M), f32),
        ],
        [
            pltpu.VMEM((ROWS, WIDTH), bf16),
            pltpu.VMEM((WIDTH, ROWS), bf16),
            pltpu.VMEM((CHIPS * 32, 128), f32),
            pltpu.VMEM((M, M), f32),
            pltpu.VMEM((16, M), f32),
            pltpu.SemaphoreType.DMA((2,)),
        ],
        specs=[SMEM, VMEM, VMEM, HBM, HBM],
        flops=4 * 4 * 1024 * 256 * 256,
        moved=2 * MIB,
        exps=MIB,
        limit=48,
    )(core, land, land_other, key, value_t)
    received = lax.ppermute(send, "ctx", swap)
    parts = call(
        combine_kernel,
        shaped((CHIPS, 16, 128), bf16),
        [pltpu.VMEM((128, 128), f32), pltpu.VMEM((128, 128), f32), pltpu.VMEM((CHIPS * 16, 128), f32)],
        n_in=2,
        flops=MIB,
        moved=MIB // 2,
    )(keep, received)
    gathered = exchange(parts)
    inverse = call(
        pinv_kernel,
        shaped((M, M), f32),
        specs=[SMEM, VMEM, VMEM],
        flops=24 * 3 * 2 * 256**3,
        moved=MIB // 2,
        exps=65536,
    )(head_id, land_q, land_k)
    mid_own = call(
        middle_kernel,
        shaped((CHIPS, 8, 128), bf16),
        [pltpu.VMEM((CHIPS * 16, 128), f32), pltpu.VMEM((8, 128), f32)],
        n_in=2,
        flops=6 * 8 * 256 * 256,
        moved=MIB // 2,
    )(gathered, inverse)
    mids = exchange(mid_own)
    kernel_f = call(
        token_kernel,
        shaped((HEADS, M, ROWS), bf16),
        n_in=2,
        flops=4 * 2 * 1024 * 256 * 256,
        moved=3 * MIB,
        exps=MIB,
    )(land_k, query)
    conv = call(
        conv_kernel,
        shaped((WIDTH, ROWS), f32),
        specs=[SMEM] + [VMEM] * 4,
        flops=2 * 512 * 768 * 512,
        moved=2 * MIB,
    )(core, value_t, near, far, conv_weight)
    mids, kernel_f, conv = lax.optimization_barrier((mids, kernel_f, conv))
    mids_other = lax.ppermute(mids, "ctx", swap)
    head_out = call(
        attend_kernel,
        [shaped((seg, WIDTH), bf16)] * groups,
        [pltpu.VMEM((CHIPS * 16, 128), f32), pltpu.VMEM((ROWS, WIDTH), bf16)],
        specs=[SMEM, SMEM] + [VMEM] * 4,
        flops=4 * 2 * 64 * 256 * 1024,
        moved=4 * MIB,
    )(core, group, mids, mids_other, kernel_f, conv)
    arrived = [head_out[0]]
    for step in range(1, groups):
        ring = [(i, (i + step) % groups) for i in range(groups)]
        arrived.append(lax.ppermute(head_out[step], "head", ring))
    return call(
        output_kernel,
        shaped((seg, w_out.shape[1]), bf16),
        specs=[SMEM] + [VMEM] * (1 + groups),
        flops=2 * 256 * 1024 * 1024,
        moved=3 * MIB,
    )(group, w_out, *arrived)


def solution(mesh):
    placed = (P("ctx", None), P(None, None, "head"), P(), P("head", None))
    return jax.shard_map(
        body, mesh=mesh, in_specs=placed, out_specs=P(("ctx", "head"), None), check_vma=False
    )
```

```python
import jax
import jax.numpy as jnp
from jax import lax
from jax.experimental import pallas as pl
from jax.experimental.pallas import tpu as pltpu
from jax.sharding import PartitionSpec as P

M = 256
NS_STEPS = 6
TAPS = 33
HALF = 16
HEADS = 4
HD = 64
WIDTH = 256
CHIPS = 32
ROWS = 1024
SCALE = 0.125
f32 = jnp.float32
bf16 = jnp.bfloat16
INTERPRET = False
VMEM = pl.BlockSpec(memory_space=pltpu.VMEM)
SMEM = pl.BlockSpec(memory_space=pltpu.SMEM)
HBM = pl.BlockSpec(memory_space=pltpu.HBM)
MIB = 1 << 20


def call(
    kernel, outs, scratch=(), specs=None, out_specs=None, n_in=1, flops=0, moved=0, exps=0, limit=24
):
    single = not isinstance(outs, (list, tuple))
    return pl.pallas_call(
        kernel,
        out_shape=outs,
        in_specs=specs or [VMEM] * n_in,
        out_specs=out_specs or (VMEM if single else [VMEM] * len(outs)),
        scratch_shapes=list(scratch),
        compiler_params=pltpu.CompilerParams(vmem_limit_bytes=limit * MIB),
        cost_estimate=pl.CostEstimate(flops=flops, bytes_accessed=moved, transcendentals=exps),
        interpret=INTERPRET,
    )


def shaped(shape, dtype):
    return jax.ShapeDtypeStruct(shape, dtype)


def dot_nn(a, b):
    return lax.dot_general(a, b, (((1,), (0,)), ((), ())), preferred_element_type=f32)


def dot_nt(a, b):
    return lax.dot_general(a, b, (((1,), (1,)), ((), ())), preferred_element_type=f32)


def split_2(x):
    high = x.astype(bf16)
    return high, (x - high.astype(f32)).astype(bf16)


def split_3(x):
    high = x.astype(bf16)
    rest = x - high.astype(f32)
    middle = rest.astype(bf16)
    return high, middle, (rest - middle.astype(f32)).astype(bf16)


def dot_wide(a, b, transposed=False):
    (ah, al), (bh, bl) = a, b
    left = jnp.concatenate([ah, ah, al], axis=1)
    if transposed:
        return dot_nt(left, jnp.concatenate([bh, bl, bh], axis=1))
    return dot_nn(left, jnp.concatenate([bh, bl, bh], axis=0))


def head_mask(head):
    lane = lax.broadcasted_iota(jnp.int32, (M, WIDTH), 1)
    return (lane >= head * HD) & (lane < (head + 1) * HD)


def landmarks_kernel(tok_hbm, w_hbm, out_ref, tok_ref, w_ref, rows_ref, sems):
    seg = ROWS // 4
    copies = [
        pltpu.make_async_copy(
            tok_hbm.at[s * seg : (s + 1) * seg, :], tok_ref.at[s * seg : (s + 1) * seg, :], sems.at[s]
        )
        for s in range(4)
    ] + [pltpu.make_async_copy(w_hbm.at[c], w_ref.at[c], sems.at[4 + c]) for c in range(2)]
    for copy in copies:
        copy.start()
    sums = []
    for s in range(4):
        copies[s].wait()
        sums.append(
            jnp.sum(tok_ref[s * seg : (s + 1) * seg, :].astype(f32), axis=0, keepdims=True)
        )
    means = jnp.concatenate(sums, axis=0) * (1.0 / seg)
    high, middle, low = split_3(means)
    stacked = jnp.concatenate(
        [high.astype(f32), middle.astype(f32), low.astype(f32), jnp.zeros_like(means)], axis=0
    ).astype(bf16)
    for kind in range(2):
        copies[4 + kind].wait()
        product = dot_nn(stacked, w_ref[kind])
        land = product[0:4] + product[4:8] + product[8:12]
        for half in range(2):
            rows_ref[pl.ds(2 * kind + half, 4, stride=4), :] = land[:, half * 128 : half * 128 + 128]
    out_ref[...] = jnp.broadcast_to(rows_ref[...].astype(bf16)[None], out_ref.shape)


def project_kernel(core_ref, own_ref, other_ref, w_ref, k_ref, vt_ref, k2_ref, vt2_ref, near_ref, far_ref):
    edges = []
    for tok_ref, key_ref, value_ref in ((own_ref, k_ref, vt_ref), (other_ref, k2_ref, vt2_ref)):
        tok = tok_ref[...]
        key_ref[...] = dot_nn(tok, w_ref[1]).astype(bf16)
        value = dot_nn(tok, w_ref[2]).astype(bf16)
        value_ref[...] = value.T
        edges.append((value[:HALF].astype(f32), value[ROWS - HALF :].astype(f32)))
    is_first = core_ref[0] == 0
    near_ref[...] = jnp.where(is_first, edges[1][0], edges[1][1]).astype(bf16)
    far_ref[...] = jnp.where(is_first, edges[0][0], edges[0][1]).astype(bf16)


def query_kernel(tok_ref, w_ref, q_ref):
    q_ref[...] = dot_nn(tok_ref[...], w_ref[0]).astype(bf16)


def pick_rows(land_rows, first, count, at):
    return jnp.concatenate(
        [land_rows[pl.ds(first + at + half, count, stride=4), :] for half in range(2)], axis=1
    )


def scores_kernel(land_ref, k_ref, vt_ref, k2_ref, vt2_ref, out_ref, land_rows):
    land_rows[...] = land_ref[...].astype(f32).reshape(CHIPS * 16, 128)
    lq = pick_rows(land_rows, 0, CHIPS * 4, 0)
    lane = lax.broadcasted_iota(jnp.int32, lq.shape, 1)
    own = [
        jnp.concatenate(
            [
                jnp.where((lane >= head * HD) & (lane < (head + 1) * HD), lq, 0.0)
                for head in (2 * pair, 2 * pair + 1)
            ],
            axis=0,
        ).astype(bf16)
        for pair in range(2)
    ]
    found = []
    for key_ref, value_ref in ((k_ref, vt_ref), (k2_ref, vt2_ref)):
        for pair in range(2):
            scores = dot_nt(key_ref[...], own[pair])
            top = jnp.max(scores, axis=0, keepdims=True)
            expo = jnp.exp((scores - top) * SCALE)
            total = jnp.sum(expo, axis=0, keepdims=True)
            rows = slice(pair * 128, pair * 128 + 128)
            found.append((top, total, dot_nn(value_ref[rows, :], expo.astype(bf16))))
    each = CHIPS // HEADS
    for pair in range(2):
        top_a, total_a, sum_a = found[pair]
        top_b, total_b, sum_b = found[2 + pair]
        top = jnp.maximum(top_a, top_b)
        scale_a = jnp.exp((top_a - top) * SCALE)
        scale_b = jnp.exp((top_b - top) * SCALE)
        total = total_a * scale_a + total_b * scale_b
        mean = sum_a * (scale_a / total) + sum_b * (scale_b / total)
        level = [p.astype(f32) for p in split_3(top * SCALE + jnp.log(total))]
        level = jnp.concatenate(level + [jnp.zeros((5, 256), f32)], axis=0)
        for side in range(2):
            lanes = slice(side * 128, side * 128 + 128)
            block = mean[side * HD : (side + 1) * HD, lanes].reshape(each, 8, 128)
            tail = jnp.broadcast_to(level[None, :, lanes], (each, 8, 128))
            at = (2 * pair + side) * each
            out_ref[at : at + each] = jnp.concatenate([block, tail], axis=1).astype(bf16)


def pinv_kernel(core_ref, head_ref, own_ref, other_ref, lk_ref, w_ref, land_rows):
    core = core_ref[0]
    count = CHIPS * 16
    land_rows[pl.ds(core * count, count), :] = own_ref[...].astype(f32).reshape(count, 128)
    land_rows[pl.ds((1 - core) * count, count), :] = other_ref[...].astype(f32).reshape(count, 128)
    lk_ref[...] = pick_rows(land_rows, 0, M, 2).astype(bf16)
    own = jnp.where(head_mask(head_ref[0]), pick_rows(land_rows, 0, M, 0), 0.0).astype(bf16)
    scores = dot_nt(own, lk_ref[...]) * SCALE
    expo = jnp.exp(scores - jnp.max(scores, axis=1, keepdims=True))
    kernel = expo / jnp.sum(expo, axis=1, keepdims=True)
    col_sum = jnp.max(jnp.sum(kernel, axis=0, keepdims=True))
    row_sum = jnp.max(jnp.sum(kernel, axis=1, keepdims=True))
    approx = kernel / (col_sum * row_sum)
    diagonal = lax.broadcasted_iota(jnp.int32, (M, M), 0) == lax.broadcasted_iota(jnp.int32, (M, M), 1)
    ident = jnp.where(diagonal, 1.0, 0.0)
    prod = dot_wide(split_2(approx), split_2(kernel), transposed=True)
    for step in range(NS_STEPS):
        parts = split_2(prod)
        square = dot_wide(parts, parts)
        last = step == NS_STEPS - 1
        right = 7.0 * ident - prod
        if not last:
            right = jnp.concatenate([right, 7.0 * prod - square], axis=1)
        both = dot_wide(split_2(square), split_2(right))
        factor = 0.25 * (13.0 * ident - 15.0 * prod + both[:, :M])
        if not last:
            prod = 0.25 * (13.0 * prod - 15.0 * square + both[:, M:])
        approx = dot_wide(split_2(factor), split_2(approx))
    w_ref[...] = approx


def middle_kernel(core_ref, own_ref, other_ref, w_ref, out_ref):
    sides = []
    for ref in (own_ref, other_ref):
        parts = ref[...].astype(f32)
        level = (parts[:, 8] + parts[:, 9]) + parts[:, 10]
        weight = jnp.exp(level - jnp.max(level, axis=0, keepdims=True))
        weight = weight / jnp.sum(weight, axis=0, keepdims=True)
        sides.append(jnp.sum(parts[:, 0:8] * weight[:, None, :], axis=0))
    is_first = core_ref[0] == 0
    bv = jnp.concatenate(
        [jnp.where(is_first, sides[0], sides[1]), jnp.where(is_first, sides[1], sides[0])], axis=1
    )
    mid = dot_wide(split_2(bv), split_2(w_ref[...]))
    rows = jnp.concatenate([mid[:, :128], mid[:, 128:]], axis=0)
    out_ref[...] = jnp.broadcast_to(rows.astype(bf16)[None], out_ref.shape)


def token_kernel(lk_ref, q_ref, out_ref):
    query = q_ref[...]
    lk = lk_ref[...].astype(f32)
    for head in range(HEADS):
        own = jnp.where(head_mask(head), lk, 0.0).astype(bf16)
        scores = dot_nt(own, query)
        expo = jnp.exp((scores - jnp.max(scores, axis=0, keepdims=True)) * SCALE)
        out_ref[head] = (expo / jnp.sum(expo, axis=0, keepdims=True)).astype(bf16)


def conv_kernel(core_ref, vt_ref, near_ref, far_ref, cw_ref, out_ref):
    blocks = ROWS // 128
    is_first = core_ref[0] == 0
    near = near_ref[...].astype(f32)
    far = far_ref[...].astype(f32)
    empty = jnp.zeros((128 - HALF, WIDTH), f32)
    before = jnp.concatenate([empty, jnp.where(is_first, far, near)], axis=0).T.astype(bf16)
    after = jnp.concatenate([jnp.where(is_first, near, far), empty], axis=0).T.astype(bf16)
    for head in range(HEADS):
        taps = jnp.concatenate([cw_ref[head : head + 1, :], jnp.zeros((1, 384 - TAPS), f32)], axis=1)
        band = pltpu.roll(
            jnp.broadcast_to(taps, (128, 384)), 128 - HALF, 1, stride=1, stride_axis=0
        )
        high, low = split_2(band)
        rows = slice(head * HD, (head + 1) * HD)
        pieces = [before[rows, :]]
        pieces += [vt_ref[rows, b * 128 : b * 128 + 128] for b in range(blocks)]
        pieces += [after[rows, :]]
        windows = jnp.concatenate(
            [jnp.concatenate(pieces[b : b + 3] * 2, axis=1) for b in range(blocks)], axis=0
        )
        out = dot_nt(windows, jnp.concatenate([high, low], axis=1))
        for b in range(blocks):
            out_ref[rows, b * 128 : b * 128 + 128] = out[b * HD : (b + 1) * HD, :]


def attend_kernel(group_ref, mid_ref, kf_ref, conv_ref, *refs):
    out_refs, joined = refs[:-1], refs[-1]
    groups = len(out_refs)
    seg = ROWS // groups
    mid = mid_ref[...].astype(f32)
    mid = jnp.concatenate(
        [mid[:, :8].reshape(M, 128), mid[:, 8:].reshape(M, 128)], axis=1
    ).astype(bf16)
    outs = []
    for head in range(HEADS):
        rows = slice(head * HD, (head + 1) * HD)
        outs.append((dot_nn(mid[rows, :], kf_ref[head]) + conv_ref[rows, :]).astype(bf16))
    joined[...] = jnp.concatenate(outs, axis=0).T
    for step in range(groups):
        to = lax.rem(group_ref[0] + step, groups)
        out_refs[step][...] = joined[pl.ds(pl.multiple_of(to * seg, seg), seg), :]


def output_kernel(group_ref, w_ref, *refs):
    x_refs, (out_hbm, joined, out_ref, sems) = refs[:-4], refs[-4:]
    groups = len(x_refs)
    for step in range(groups):
        source = lax.rem(group_ref[0] + groups - step, groups)
        joined[:, pl.ds(pl.multiple_of(source * WIDTH, WIDTH), WIDTH)] = x_refs[step][...]
    copies = []
    for part in range(4):
        lanes = slice(part * 256, part * 256 + 256)
        out_ref[:, lanes] = dot_nn(joined[...], w_ref[:, lanes]).astype(bf16)
        copies.append(pltpu.make_async_copy(out_ref.at[:, lanes], out_hbm.at[:, lanes], sems.at[part]))
        copies[-1].start()
    for copy in copies:
        copy.wait()


def body(tokens, w_qkv, w_out, conv_weight):
    groups = lax.axis_size("head")
    same_core = [[2 * chip + core for chip in range(CHIPS)] for core in range(2)]
    swap = [(i, i ^ 1) for i in range(2 * CHIPS)]
    onward = [(2 * chip + 1, 2 * chip + 2) for chip in range(CHIPS - 1)]
    onward += [(b, a) for a, b in onward]
    place = lax.axis_index("ctx").astype(jnp.int32)
    group = lax.axis_index("head").astype(jnp.int32).reshape(1)
    seg = ROWS // groups
    core = (place % 2).reshape(1)
    head_id = (place // (2 * CHIPS // HEADS)).reshape(1)

    def exchange(x):
        return lax.all_to_all(x, "ctx", 0, 0, tiled=True, axis_index_groups=same_core)

    tokens_other = lax.ppermute(tokens, "ctx", swap)
    own = call(
        landmarks_kernel,
        shaped((CHIPS, 16, 128), bf16),
        [
            pltpu.VMEM((ROWS, 1024), bf16),
            pltpu.VMEM((2, 1024, WIDTH), bf16),
            pltpu.VMEM((16, 128), f32),
            pltpu.SemaphoreType.DMA((6,)),
        ],
        specs=[HBM, HBM],
        flops=2 * 16 * 1024 * 512,
        moved=3 * MIB,
        limit=63,
    )(tokens, w_qkv)
    land = exchange(own)
    key, value_t, key_other, value_other, near, far = call(
        project_kernel,
        [shaped((ROWS, WIDTH), bf16), shaped((WIDTH, ROWS), bf16)] * 2
        + [shaped((HALF, WIDTH), bf16)] * 2,
        specs=[SMEM, VMEM, VMEM, VMEM],
        flops=4 * 1024 * 1024 * 512,
        moved=8 * MIB,
    )(core, tokens, tokens_other, w_qkv)
    land, key, value_t, near, far, key_other, value_other = lax.optimization_barrier(
        (land, key, value_t, near, far, key_other, value_other)
    )
    parts = call(
        scores_kernel,
        shaped((CHIPS, 16, 128), bf16),
        [pltpu.VMEM((CHIPS * 16, 128), f32)],
        n_in=5,
        flops=4 * 4 * 1024 * 256 * 256,
        moved=4 * MIB,
        exps=MIB,
    )(land, key, value_t, key_other, value_other)
    gathered = exchange(parts)
    land, parts = lax.optimization_barrier((land, parts))
    land_other = lax.ppermute(land, "ctx", swap)
    land_k, inverse = call(
        pinv_kernel,
        [shaped((M, WIDTH), bf16), shaped((M, M), f32)],
        [pltpu.VMEM((CHIPS * 32, 128), f32)],
        specs=[SMEM, SMEM, VMEM, VMEM],
        flops=24 * 3 * 2 * 256**3,
        moved=MIB // 2,
        exps=65536,
    )(core, head_id, land, land_other)
    late_tokens, late_w, inverse = lax.optimization_barrier((tokens, w_qkv, inverse))
    query = call(
        query_kernel,
        shaped((ROWS, WIDTH), bf16),
        n_in=2,
        flops=2 * 1024 * 1024 * 256,
        moved=4 * MIB,
    )(late_tokens, late_w)
    gathered, query = lax.optimization_barrier((gathered, query))
    gathered_other = lax.ppermute(gathered, "ctx", swap)
    mid_own = call(
        middle_kernel,
        shaped((CHIPS, 16, 128), bf16),
        specs=[SMEM] + [VMEM] * 3,
        flops=6 * 8 * 256 * 256,
        moved=MIB // 2,
    )(core, gathered, gathered_other, inverse)
    mids = exchange(mid_own)
    far = lax.ppermute(far, "ctx", onward)
    kernel_f = call(
        token_kernel,
        shaped((HEADS, M, ROWS), bf16),
        n_in=2,
        flops=4 * 2 * 1024 * 256 * 256,
        moved=3 * MIB,
        exps=MIB,
    )(land_k, query)
    far, kernel_f = lax.optimization_barrier((far, kernel_f))
    conv = call(
        conv_kernel,
        shaped((WIDTH, ROWS), f32),
        specs=[SMEM] + [VMEM] * 4,
        flops=2 * 512 * 768 * 512,
        moved=2 * MIB,
    )(core, value_t, near, far, conv_weight)
    mids, kernel_f, conv = lax.optimization_barrier((mids, kernel_f, conv))
    head_out = call(
        attend_kernel,
        [shaped((seg, WIDTH), bf16)] * groups,
        [pltpu.VMEM((ROWS, WIDTH), bf16)],
        specs=[SMEM] + [VMEM] * 3,
        flops=4 * 2 * 64 * 256 * 1024,
        moved=4 * MIB,
    )(group, mids, kernel_f, conv)
    arrived = [head_out[0]]
    for step in range(1, groups):
        ring = [(i, (i + step) % groups) for i in range(groups)]
        arrived.append(lax.ppermute(head_out[step], "head", ring))
    return call(
        output_kernel,
        shaped((seg, w_out.shape[1]), bf16),
        [
            pltpu.VMEM((seg, w_out.shape[0]), bf16),
            pltpu.VMEM((seg, w_out.shape[1]), bf16),
            pltpu.SemaphoreType.DMA((4,)),
        ],
        specs=[SMEM] + [VMEM] * (1 + groups),
        out_specs=HBM,
        flops=2 * 256 * 1024 * 1024,
        moved=3 * MIB,
    )(group, w_out, *arrived)


def solution(mesh):
    placed = (P("ctx", None), P(None, None, "head"), P(), P("head", None))
    return jax.shard_map(
        body, mesh=mesh, in_specs=placed, out_specs=P(("ctx", "head"), None), check_vma=False
    )
```

```python
import jax
import jax.numpy as jnp
from jax import lax
from jax.experimental import pallas as pl
from jax.experimental.pallas import tpu as pltpu
from jax.sharding import PartitionSpec as P

M = 256
NS_STEPS = 6
TAPS = 33
HALF = 16
HEADS = 4
HD = 64
WIDTH = 256
CHIPS = 32
ROWS = 1024
SCALE = 0.125
LOG2_E = 1.4426950408889634
f32 = jnp.float32
bf16 = jnp.bfloat16
INTERPRET = False
VMEM = pl.BlockSpec(memory_space=pltpu.VMEM)
SMEM = pl.BlockSpec(memory_space=pltpu.SMEM)
HBM = pl.BlockSpec(memory_space=pltpu.HBM)
MIB = 1 << 20


def call(
    kernel, outs, scratch=(), specs=None, out_specs=None, n_in=1, flops=0, moved=0, exps=0, limit=24
):
    single = not isinstance(outs, (list, tuple))
    return pl.pallas_call(
        kernel,
        out_shape=outs,
        in_specs=specs or [VMEM] * n_in,
        out_specs=out_specs or (VMEM if single else [VMEM] * len(outs)),
        scratch_shapes=list(scratch),
        compiler_params=pltpu.CompilerParams(vmem_limit_bytes=limit * MIB),
        cost_estimate=pl.CostEstimate(flops=flops, bytes_accessed=moved, transcendentals=exps),
        interpret=INTERPRET,
    )


def shaped(shape, dtype):
    return jax.ShapeDtypeStruct(shape, dtype)


def dot_nn(a, b):
    return lax.dot_general(a, b, (((1,), (0,)), ((), ())), preferred_element_type=f32)


def dot_nt(a, b):
    return lax.dot_general(a, b, (((1,), (1,)), ((), ())), preferred_element_type=f32)


def split_2(x):
    high = x.astype(bf16)
    return high, (x - high.astype(f32)).astype(bf16)


def split_3(x):
    high = x.astype(bf16)
    rest = x - high.astype(f32)
    middle = rest.astype(bf16)
    return high, middle, (rest - middle.astype(f32)).astype(bf16)


def dot_wide(a, b, transposed=False):
    (ah, al), (bh, bl) = a, b
    left = jnp.concatenate([ah, ah, al], axis=1)
    if transposed:
        return dot_nt(left, jnp.concatenate([bh, bl, bh], axis=1))
    return dot_nn(left, jnp.concatenate([bh, bl, bh], axis=0))


def head_mask(head):
    lane = lax.broadcasted_iota(jnp.int32, (M, WIDTH), 1)
    return (lane >= head * HD) & (lane < (head + 1) * HD)


def landmarks_kernel(tok_hbm, w_hbm, out_ref, tok_ref, w_ref, rows_ref, sems):
    seg = ROWS // 4
    copies = [
        pltpu.make_async_copy(
            tok_hbm.at[s * seg : (s + 1) * seg, :], tok_ref.at[s * seg : (s + 1) * seg, :], sems.at[s]
        )
        for s in range(4)
    ] + [pltpu.make_async_copy(w_hbm.at[c], w_ref.at[c], sems.at[4 + c]) for c in range(2)]
    for copy in copies:
        copy.start()
    sums = []
    for s in range(4):
        copies[s].wait()
        sums.append(
            jnp.sum(tok_ref[s * seg : (s + 1) * seg, :].astype(f32), axis=0, keepdims=True)
        )
    means = jnp.concatenate(sums, axis=0) * (1.0 / seg)
    high, middle, low = split_3(means)
    stacked = jnp.concatenate(
        [high.astype(f32), middle.astype(f32), low.astype(f32), jnp.zeros_like(means)], axis=0
    ).astype(bf16)
    for kind in range(2):
        copies[4 + kind].wait()
        product = dot_nn(stacked, w_ref[kind])
        land = product[0:4] + product[4:8] + product[8:12]
        for half in range(2):
            rows_ref[pl.ds(2 * kind + half, 4, stride=4), :] = land[:, half * 128 : half * 128 + 128]
    out_ref[...] = jnp.broadcast_to(rows_ref[...].astype(bf16)[None], out_ref.shape)


def project_kernel(
    core_ref,
    own_hbm,
    other_hbm,
    w_hbm,
    k_ref,
    vt_ref,
    k2_ref,
    vt2_ref,
    near_ref,
    far_ref,
    tok_ref,
    w_ref,
    sems,
):
    cut = ROWS // 4
    loads = [pltpu.make_async_copy(w_hbm.at[1 + c], w_ref.at[c], sems.at[8 + c]) for c in range(2)]
    copies = [
        pltpu.make_async_copy(
            source.at[s * cut : (s + 1) * cut, :],
            tok_ref.at[side, s * cut : (s + 1) * cut, :],
            sems.at[4 * side + s],
        )
        for side, source in enumerate((own_hbm, other_hbm))
        for s in range(4)
    ]
    for copy in loads + copies:
        copy.start()
    for copy in loads:
        copy.wait()
    edges = []
    for side, (key_ref, value_ref) in enumerate(((k_ref, vt_ref), (k2_ref, vt2_ref))):
        for s in range(4):
            copies[4 * side + s].wait()
            rows = slice(s * cut, (s + 1) * cut)
            tok = tok_ref[side, rows, :]
            key_ref[rows, :] = dot_nn(tok, w_ref[0]).astype(bf16)
            value = dot_nn(tok, w_ref[1]).astype(bf16)
            value_ref[:, rows] = value.T
            edges.append(value)
    is_first = core_ref[0] == 0
    first, last = edges[0][:HALF].astype(f32), edges[3][cut - HALF :].astype(f32)
    far_ref[...] = jnp.where(is_first, first, last).astype(bf16)
    first, last = edges[4][:HALF].astype(f32), edges[7][cut - HALF :].astype(f32)
    near_ref[...] = jnp.where(is_first, first, last).astype(bf16)


def query_kernel(tok_ref, w_ref, q_ref):
    q_ref[...] = dot_nn(tok_ref[...], w_ref[0]).astype(bf16)


def pick_rows(land_rows, first, count, at):
    return jnp.concatenate(
        [land_rows[pl.ds(first + at + half, count, stride=4), :] for half in range(2)], axis=1
    )


def scores_kernel(land_ref, k_ref, vt_ref, k2_ref, vt2_ref, out_ref, land_rows):
    land_rows[...] = land_ref[...].astype(f32).reshape(CHIPS * 16, 128)
    lq = pick_rows(land_rows, 0, CHIPS * 4, 0)
    lane = lax.broadcasted_iota(jnp.int32, lq.shape, 1)
    own = [
        jnp.concatenate(
            [
                jnp.where((lane >= head * HD) & (lane < (head + 1) * HD), lq, 0.0)
                for head in (2 * pair, 2 * pair + 1)
            ],
            axis=0,
        ).astype(bf16)
        for pair in range(2)
    ]
    found = []
    keys, values = (k_ref, k2_ref), (vt_ref, vt2_ref)
    ahead = dot_nt(keys[0][...], own[0])
    for step in range(4):
        side, pair = step // 2, step % 2
        scores = ahead
        if step < 3:
            ahead = dot_nt(keys[(step + 1) // 2][...], own[1 - pair])
        top = jnp.max(scores, axis=0, keepdims=True)
        expo = jnp.exp2((scores - top) * (SCALE * LOG2_E))
        total = jnp.sum(expo, axis=0, keepdims=True)
        rows = slice(pair * 128, pair * 128 + 128)
        found.append((top, total, dot_nn(values[side][rows, :], expo.astype(bf16))))
    each = CHIPS // HEADS
    for pair in range(2):
        top_a, total_a, sum_a = found[pair]
        top_b, total_b, sum_b = found[2 + pair]
        top = jnp.maximum(top_a, top_b)
        scale_a = jnp.exp((top_a - top) * SCALE)
        scale_b = jnp.exp((top_b - top) * SCALE)
        total = total_a * scale_a + total_b * scale_b
        mean = sum_a * (scale_a / total) + sum_b * (scale_b / total)
        level = [p.astype(f32) for p in split_3(top * SCALE + jnp.log(total))]
        level = jnp.concatenate(level + [jnp.zeros((5, 256), f32)], axis=0)
        for side in range(2):
            lanes = slice(side * 128, side * 128 + 128)
            block = mean[side * HD : (side + 1) * HD, lanes].reshape(each, 8, 128)
            tail = jnp.broadcast_to(level[None, :, lanes], (each, 8, 128))
            at = (2 * pair + side) * each
            out_ref[at : at + each] = jnp.concatenate([block, tail], axis=1).astype(bf16)


def pinv_kernel(core_ref, head_ref, own_ref, other_ref, lk_ref, w_ref, land_rows):
    core = core_ref[0]
    count = CHIPS * 16
    land_rows[pl.ds(core * count, count), :] = own_ref[...].astype(f32).reshape(count, 128)
    land_rows[pl.ds((1 - core) * count, count), :] = other_ref[...].astype(f32).reshape(count, 128)
    lk_ref[...] = pick_rows(land_rows, 0, M, 2).astype(bf16)
    own = jnp.where(head_mask(head_ref[0]), pick_rows(land_rows, 0, M, 0), 0.0).astype(bf16)
    scores = dot_nt(own, lk_ref[...]) * SCALE
    expo = jnp.exp(scores - jnp.max(scores, axis=1, keepdims=True))
    kernel = expo / jnp.sum(expo, axis=1, keepdims=True)
    col_sum = jnp.max(jnp.sum(kernel, axis=0, keepdims=True))
    row_sum = jnp.max(jnp.sum(kernel, axis=1, keepdims=True))
    approx = kernel / (col_sum * row_sum)
    diagonal = lax.broadcasted_iota(jnp.int32, (M, M), 0) == lax.broadcasted_iota(jnp.int32, (M, M), 1)
    ident = jnp.where(diagonal, 1.0, 0.0)
    prod = dot_wide(split_2(approx), split_2(kernel), transposed=True)
    for step in range(NS_STEPS):
        parts = split_2(prod)
        square = dot_wide(parts, parts)
        last = step == NS_STEPS - 1
        right = 7.0 * ident - prod
        if not last:
            right = jnp.concatenate([right, 7.0 * prod - square], axis=1)
        both = dot_wide(split_2(square), split_2(right))
        factor = 0.25 * (13.0 * ident - 15.0 * prod + both[:, :M])
        if not last:
            prod = 0.25 * (13.0 * prod - 15.0 * square + both[:, M:])
        approx = dot_wide(split_2(factor), split_2(approx))
    w_ref[...] = approx


def reduce_kernel(parts_ref, out_ref):
    parts = parts_ref[...].astype(f32)
    level = (parts[:, 8] + parts[:, 9]) + parts[:, 10]
    weight = jnp.exp(level - jnp.max(level, axis=0, keepdims=True))
    weight = weight / jnp.sum(weight, axis=0, keepdims=True)
    out_ref[...] = jnp.sum(parts[:, 0:8] * weight[:, None, :], axis=0)


def middle_kernel(core_ref, own_ref, other_ref, w_ref, out_ref):
    own, other = own_ref[...], other_ref[...]
    is_first = core_ref[0] == 0
    bv = jnp.concatenate([jnp.where(is_first, own, other), jnp.where(is_first, other, own)], axis=1)
    mid = dot_wide(split_2(bv), split_2(w_ref[...]))
    rows = jnp.concatenate([mid[:, :128], mid[:, 128:]], axis=0)
    out_ref[...] = jnp.broadcast_to(rows.astype(bf16)[None], out_ref.shape)


def token_kernel(lk_ref, q_ref, out_ref):
    query = q_ref[...]
    lk = lk_ref[...].astype(f32)
    for head in range(HEADS):
        own = jnp.where(head_mask(head), lk, 0.0).astype(bf16)
        scores = dot_nt(own, query)
        expo = jnp.exp2((scores - jnp.max(scores, axis=0, keepdims=True)) * (SCALE * LOG2_E))
        out_ref[head] = (expo * (1.0 / jnp.sum(expo, axis=0, keepdims=True))).astype(bf16)


def conv_kernel(core_ref, vt_ref, near_ref, far_ref, cw_ref, out_ref):
    blocks = ROWS // 128
    is_first = core_ref[0] == 0
    near = near_ref[...].astype(f32)
    far = far_ref[...].astype(f32)
    empty = jnp.zeros((128 - HALF, WIDTH), f32)
    before = jnp.concatenate([empty, jnp.where(is_first, far, near)], axis=0).T.astype(bf16)
    after = jnp.concatenate([jnp.where(is_first, near, far), empty], axis=0).T.astype(bf16)
    for head in range(HEADS):
        taps = jnp.concatenate([cw_ref[head : head + 1, :], jnp.zeros((1, 384 - TAPS), f32)], axis=1)
        band = pltpu.roll(
            jnp.broadcast_to(taps, (128, 384)), 128 - HALF, 1, stride=1, stride_axis=0
        )
        high, low = split_2(band)
        rows = slice(head * HD, (head + 1) * HD)
        pieces = [before[rows, :]]
        pieces += [vt_ref[rows, b * 128 : b * 128 + 128] for b in range(blocks)]
        pieces += [after[rows, :]]
        windows = jnp.concatenate(
            [jnp.concatenate(pieces[b : b + 3] * 2, axis=1) for b in range(blocks)], axis=0
        )
        out = dot_nt(windows, jnp.concatenate([high, low], axis=1))
        for b in range(blocks):
            out_ref[rows, b * 128 : b * 128 + 128] = out[b * HD : (b + 1) * HD, :]


def attend_kernel(group_ref, mid_ref, kf_ref, conv_ref, *refs):
    out_refs, joined = refs[:-1], refs[-1]
    groups = len(out_refs)
    seg = ROWS // groups
    mid = mid_ref[...].astype(f32)
    mid = jnp.concatenate(
        [mid[:, :8].reshape(M, 128), mid[:, 8:].reshape(M, 128)], axis=1
    ).astype(bf16)
    outs = []
    for head in range(HEADS):
        rows = slice(head * HD, (head + 1) * HD)
        outs.append((dot_nn(mid[rows, :], kf_ref[head]) + conv_ref[rows, :]).astype(bf16))
    joined[...] = jnp.concatenate(outs, axis=0).T
    for step in range(groups):
        to = lax.rem(group_ref[0] + step, groups)
        out_refs[step][...] = joined[pl.ds(pl.multiple_of(to * seg, seg), seg), :]


def output_kernel(group_ref, w_ref, *refs):
    x_refs, (out_hbm, joined, out_ref, sems) = refs[:-4], refs[-4:]
    groups = len(x_refs)
    for step in range(groups):
        source = lax.rem(group_ref[0] + groups - step, groups)
        joined[:, pl.ds(pl.multiple_of(source * WIDTH, WIDTH), WIDTH)] = x_refs[step][...]
    copies = []
    for part in range(4):
        lanes = slice(part * 256, part * 256 + 256)
        out_ref[:, lanes] = dot_nn(joined[...], w_ref[:, lanes]).astype(bf16)
        copies.append(pltpu.make_async_copy(out_ref.at[:, lanes], out_hbm.at[:, lanes], sems.at[part]))
        copies[-1].start()
    for copy in copies:
        copy.wait()


def body(tokens, w_qkv, w_out, conv_weight):
    groups = lax.axis_size("head")
    same_core = [[2 * chip + core for chip in range(CHIPS)] for core in range(2)]
    swap = [(i, i ^ 1) for i in range(2 * CHIPS)]
    onward = [(2 * chip + 1, 2 * chip + 2) for chip in range(CHIPS - 1)]
    onward += [(b, a) for a, b in onward]
    place = lax.axis_index("ctx").astype(jnp.int32)
    group = lax.axis_index("head").astype(jnp.int32).reshape(1)
    seg = ROWS // groups
    core = (place % 2).reshape(1)
    head_id = (place // (2 * CHIPS // HEADS)).reshape(1)

    def exchange(x):
        return lax.all_to_all(x, "ctx", 0, 0, tiled=True, axis_index_groups=same_core)

    tokens_other = lax.ppermute(tokens, "ctx", swap)
    own = call(
        landmarks_kernel,
        shaped((CHIPS, 16, 128), bf16),
        [
            pltpu.VMEM((ROWS, 1024), bf16),
            pltpu.VMEM((2, 1024, WIDTH), bf16),
            pltpu.VMEM((16, 128), f32),
            pltpu.SemaphoreType.DMA((6,)),
        ],
        specs=[HBM, HBM],
        flops=2 * 16 * 1024 * 512,
        moved=3 * MIB,
        limit=63,
    )(tokens, w_qkv)
    land = exchange(own)
    key, value_t, key_other, value_other, near, far = call(
        project_kernel,
        [shaped((ROWS, WIDTH), bf16), shaped((WIDTH, ROWS), bf16)] * 2
        + [shaped((HALF, WIDTH), bf16)] * 2,
        [
            pltpu.VMEM((2, ROWS, 1024), bf16),
            pltpu.VMEM((2, 1024, WIDTH), bf16),
            pltpu.SemaphoreType.DMA((10,)),
        ],
        specs=[SMEM, HBM, HBM, HBM],
        limit=51,
        flops=4 * 1024 * 1024 * 512,
        moved=8 * MIB,
    )(core, tokens, tokens_other, w_qkv)
    land, key, value_t, near, far, key_other, value_other = lax.optimization_barrier(
        (land, key, value_t, near, far, key_other, value_other)
    )
    parts = call(
        scores_kernel,
        shaped((CHIPS, 16, 128), bf16),
        [pltpu.VMEM((CHIPS * 16, 128), f32)],
        n_in=5,
        flops=4 * 4 * 1024 * 256 * 256,
        moved=4 * MIB,
        exps=MIB,
    )(land, key, value_t, key_other, value_other)
    gathered = exchange(parts)
    land, parts = lax.optimization_barrier((land, parts))
    land_other = lax.ppermute(land, "ctx", swap)
    land_k, inverse = call(
        pinv_kernel,
        [shaped((M, WIDTH), bf16), shaped((M, M), f32)],
        [pltpu.VMEM((CHIPS * 32, 128), f32)],
        specs=[SMEM, SMEM, VMEM, VMEM],
        flops=24 * 3 * 2 * 256**3,
        moved=MIB // 2,
        exps=65536,
    )(core, head_id, land, land_other)
    late_tokens, late_w, inverse = lax.optimization_barrier((tokens, w_qkv, inverse))
    query = call(
        query_kernel,
        shaped((ROWS, WIDTH), bf16),
        n_in=2,
        flops=2 * 1024 * 1024 * 256,
        moved=4 * MIB,
    )(late_tokens, late_w)
    gathered, query = lax.optimization_barrier((gathered, query))
    reduced = call(
        reduce_kernel, shaped((8, 128), f32), flops=32 * 8 * 128 * 2, moved=MIB // 8
    )(gathered)
    reduced_other = lax.ppermute(reduced, "ctx", swap)
    mid_own = call(
        middle_kernel,
        shaped((CHIPS, 16, 128), bf16),
        specs=[SMEM] + [VMEM] * 3,
        flops=6 * 8 * 256 * 256,
        moved=MIB // 2,
    )(core, reduced, reduced_other, inverse)
    mids = exchange(mid_own)
    far = lax.ppermute(far, "ctx", onward)
    kernel_f = call(
        token_kernel,
        shaped((HEADS, M, ROWS), bf16),
        n_in=2,
        flops=4 * 2 * 1024 * 256 * 256,
        moved=3 * MIB,
        exps=MIB,
    )(land_k, query)
    far, kernel_f = lax.optimization_barrier((far, kernel_f))
    conv = call(
        conv_kernel,
        shaped((WIDTH, ROWS), f32),
        specs=[SMEM] + [VMEM] * 4,
        flops=2 * 512 * 768 * 512,
        moved=2 * MIB,
    )(core, value_t, near, far, conv_weight)
    mids, kernel_f, conv = lax.optimization_barrier((mids, kernel_f, conv))
    head_out = call(
        attend_kernel,
        [shaped((seg, WIDTH), bf16)] * groups,
        [pltpu.VMEM((ROWS, WIDTH), bf16)],
        specs=[SMEM] + [VMEM] * 3,
        flops=4 * 2 * 64 * 256 * 1024,
        moved=4 * MIB,
    )(group, mids, kernel_f, conv)
    arrived = [head_out[0]]
    for step in range(1, groups):
        ring = [(i, (i + step) % groups) for i in range(groups)]
        arrived.append(lax.ppermute(head_out[step], "head", ring))
    return call(
        output_kernel,
        shaped((seg, w_out.shape[1]), bf16),
        [
            pltpu.VMEM((seg, w_out.shape[0]), bf16),
            pltpu.VMEM((seg, w_out.shape[1]), bf16),
            pltpu.SemaphoreType.DMA((4,)),
        ],
        specs=[SMEM] + [VMEM] * (1 + groups),
        out_specs=HBM,
        flops=2 * 256 * 1024 * 1024,
        moved=3 * MIB,
    )(group, w_out, *arrived)


def solution(mesh):
    placed = (P("ctx", None), P(None, None, "head"), P(), P("head", None))
    return jax.shard_map(
        body, mesh=mesh, in_specs=placed, out_specs=P(("ctx", "head"), None), check_vma=False
    )
```

```python
import jax
import jax.numpy as jnp
from jax import lax
from jax.experimental import pallas as pl
from jax.experimental.pallas import tpu as pltpu
from jax.sharding import PartitionSpec as P

M = 256
NS_STEPS = 6
TAPS = 33
HALF = 16
HEADS = 4
HD = 64
WIDTH = 256
CHIPS = 32
ROWS = 1024
SCALE = 0.125
LOG2_E = 1.4426950408889634
f32 = jnp.float32
bf16 = jnp.bfloat16
INTERPRET = False
VMEM = pl.BlockSpec(memory_space=pltpu.VMEM)
SMEM = pl.BlockSpec(memory_space=pltpu.SMEM)
HBM = pl.BlockSpec(memory_space=pltpu.HBM)
MIB = 1 << 20


def call(
    kernel, outs, scratch=(), specs=None, out_specs=None, n_in=1, flops=0, moved=0, exps=0, limit=24
):
    single = not isinstance(outs, (list, tuple))
    return pl.pallas_call(
        kernel,
        out_shape=outs,
        in_specs=specs or [VMEM] * n_in,
        out_specs=out_specs or (VMEM if single else [VMEM] * len(outs)),
        scratch_shapes=list(scratch),
        compiler_params=pltpu.CompilerParams(vmem_limit_bytes=limit * MIB),
        cost_estimate=pl.CostEstimate(flops=flops, bytes_accessed=moved, transcendentals=exps),
        interpret=INTERPRET,
    )


def shaped(shape, dtype):
    return jax.ShapeDtypeStruct(shape, dtype)


def dot_nn(a, b):
    return lax.dot_general(a, b, (((1,), (0,)), ((), ())), preferred_element_type=f32)


def dot_nt(a, b):
    return lax.dot_general(a, b, (((1,), (1,)), ((), ())), preferred_element_type=f32)


def split_2(x):
    high = x.astype(bf16)
    return high, (x - high.astype(f32)).astype(bf16)


def split_3(x):
    high = x.astype(bf16)
    rest = x - high.astype(f32)
    middle = rest.astype(bf16)
    return high, middle, (rest - middle.astype(f32)).astype(bf16)


def dot_wide(a, b, transposed=False):
    (ah, al), (bh, bl) = a, b
    left = jnp.concatenate([ah, ah, al], axis=1)
    if transposed:
        return dot_nt(left, jnp.concatenate([bh, bl, bh], axis=1))
    return dot_nn(left, jnp.concatenate([bh, bl, bh], axis=0))


def head_mask(head):
    lane = lax.broadcasted_iota(jnp.int32, (M, WIDTH), 1)
    return (lane >= head * HD) & (lane < (head + 1) * HD)


def landmarks_kernel(tok_hbm, w_hbm, out_ref, tok_ref, w_ref, rows_ref, sems):
    seg = ROWS // 4
    copies = [
        pltpu.make_async_copy(
            tok_hbm.at[s * seg : (s + 1) * seg, :], tok_ref.at[s * seg : (s + 1) * seg, :], sems.at[s]
        )
        for s in range(4)
    ] + [pltpu.make_async_copy(w_hbm.at[c], w_ref.at[c], sems.at[4 + c]) for c in range(2)]
    for copy in copies:
        copy.start()
    sums = []
    for s in range(4):
        copies[s].wait()
        sums.append(
            jnp.sum(tok_ref[s * seg : (s + 1) * seg, :].astype(f32), axis=0, keepdims=True)
        )
    means = jnp.concatenate(sums, axis=0) * (1.0 / seg)
    high, low = split_2(means)
    stacked = jnp.concatenate([high.astype(f32), low.astype(f32)], axis=0).astype(bf16)
    for kind in range(2):
        copies[4 + kind].wait()
        product = dot_nn(stacked, w_ref[kind])
        land = product[0:4] + product[4:8]
        for half in range(2):
            rows_ref[pl.ds(2 * kind + half, 4, stride=4), :] = land[:, half * 128 : half * 128 + 128]
    out_ref[...] = jnp.broadcast_to(rows_ref[...].astype(bf16)[None], out_ref.shape)


def project_kernel(
    core_ref,
    own_hbm,
    other_hbm,
    w_hbm,
    k_ref,
    vt_ref,
    k2_ref,
    vt2_ref,
    near_ref,
    far_ref,
    tok_ref,
    w_ref,
    sems,
):
    cut = ROWS // 4
    loads = [pltpu.make_async_copy(w_hbm.at[1 + c], w_ref.at[c], sems.at[8 + c]) for c in range(2)]
    copies = [
        pltpu.make_async_copy(
            source.at[s * cut : (s + 1) * cut, :],
            tok_ref.at[side, s * cut : (s + 1) * cut, :],
            sems.at[4 * side + s],
        )
        for side, source in enumerate((own_hbm, other_hbm))
        for s in range(4)
    ]
    for copy in loads + copies:
        copy.start()
    for copy in loads:
        copy.wait()
    edges = []
    for side, (key_ref, value_ref) in enumerate(((k_ref, vt_ref), (k2_ref, vt2_ref))):
        for s in range(4):
            copies[4 * side + s].wait()
            rows = slice(s * cut, (s + 1) * cut)
            tok = tok_ref[side, rows, :]
            key_ref[rows, :] = dot_nn(tok, w_ref[0]).astype(bf16)
            value = dot_nn(tok, w_ref[1]).astype(bf16)
            value_ref[:, rows] = value.T
            edges.append(value)
    is_first = core_ref[0] == 0
    first, last = edges[0][:HALF].astype(f32), edges[3][cut - HALF :].astype(f32)
    far_ref[...] = jnp.where(is_first, first, last).astype(bf16)
    first, last = edges[4][:HALF].astype(f32), edges[7][cut - HALF :].astype(f32)
    near_ref[...] = jnp.where(is_first, first, last).astype(bf16)


def query_kernel(tok_ref, w_ref, q_ref):
    q_ref[...] = dot_nn(tok_ref[...], w_ref[0]).astype(bf16)


def pick_rows(land_rows, first, count, at):
    return jnp.concatenate(
        [land_rows[pl.ds(first + at + half, count, stride=4), :] for half in range(2)], axis=1
    )


def scores_kernel(land_ref, k_ref, vt_ref, k2_ref, vt2_ref, out_ref, land_rows):
    land_rows[...] = land_ref[...].astype(f32).reshape(CHIPS * 16, 128)
    lq = pick_rows(land_rows, 0, CHIPS * 4, 0)
    lane = lax.broadcasted_iota(jnp.int32, lq.shape, 1)
    own = [
        jnp.concatenate(
            [
                jnp.where((lane >= head * HD) & (lane < (head + 1) * HD), lq, 0.0)
                for head in (2 * pair, 2 * pair + 1)
            ],
            axis=0,
        ).astype(bf16)
        for pair in range(2)
    ]
    found = []
    keys, values = (k_ref, k2_ref), (vt_ref, vt2_ref)
    ahead = dot_nt(keys[0][...], own[0])
    for step in range(4):
        side, pair = step // 2, step % 2
        scores = ahead
        if step < 3:
            ahead = dot_nt(keys[(step + 1) // 2][...], own[1 - pair])
        top = jnp.max(scores, axis=0, keepdims=True)
        expo = jnp.exp2((scores - top) * (SCALE * LOG2_E))
        total = jnp.sum(expo, axis=0, keepdims=True)
        rows = slice(pair * 128, pair * 128 + 128)
        found.append((top, total, dot_nn(values[side][rows, :], expo.astype(bf16))))
    each = CHIPS // HEADS
    for pair in range(2):
        top_a, total_a, sum_a = found[pair]
        top_b, total_b, sum_b = found[2 + pair]
        top = jnp.maximum(top_a, top_b)
        scale_a = jnp.exp((top_a - top) * SCALE)
        scale_b = jnp.exp((top_b - top) * SCALE)
        total = total_a * scale_a + total_b * scale_b
        mean = sum_a * (scale_a / total) + sum_b * (scale_b / total)
        level = [p.astype(f32) for p in split_3(top * SCALE + jnp.log(total))]
        level = jnp.concatenate(level + [jnp.zeros((5, 256), f32)], axis=0)
        for side in range(2):
            lanes = slice(side * 128, side * 128 + 128)
            block = mean[side * HD : (side + 1) * HD, lanes].reshape(each, 8, 128)
            tail = jnp.broadcast_to(level[None, :, lanes], (each, 8, 128))
            at = (2 * pair + side) * each
            out_ref[at : at + each] = jnp.concatenate([block, tail], axis=1).astype(bf16)


def pinv_kernel(core_ref, head_ref, own_ref, other_ref, lk_ref, w_ref, land_rows):
    core = core_ref[0]
    count = CHIPS * 16
    land_rows[pl.ds(core * count, count), :] = own_ref[...].astype(f32).reshape(count, 128)
    land_rows[pl.ds((1 - core) * count, count), :] = other_ref[...].astype(f32).reshape(count, 128)
    lk_ref[...] = pick_rows(land_rows, 0, M, 2).astype(bf16)
    own = jnp.where(head_mask(head_ref[0]), pick_rows(land_rows, 0, M, 0), 0.0).astype(bf16)
    scores = dot_nt(own, lk_ref[...]) * SCALE
    expo = jnp.exp(scores - jnp.max(scores, axis=1, keepdims=True))
    kernel = expo / jnp.sum(expo, axis=1, keepdims=True)
    col_sum = jnp.max(jnp.sum(kernel, axis=0, keepdims=True))
    row_sum = jnp.max(jnp.sum(kernel, axis=1, keepdims=True))
    approx = kernel / (col_sum * row_sum)
    diagonal = lax.broadcasted_iota(jnp.int32, (M, M), 0) == lax.broadcasted_iota(jnp.int32, (M, M), 1)
    ident = jnp.where(diagonal, 1.0, 0.0)
    prod = dot_wide(split_2(approx), split_2(kernel), transposed=True)
    factor = None
    for step in range(NS_STEPS):
        parts = split_2(prod)
        square = dot_wide(parts, parts)
        if factor is not None:
            approx = dot_wide(split_2(factor), split_2(approx))
        last = step == NS_STEPS - 1
        right = 7.0 * ident - prod
        if not last:
            right = jnp.concatenate([right, 7.0 * prod - square], axis=1)
        both = dot_wide(split_2(square), split_2(right))
        factor = 0.25 * (13.0 * ident - 15.0 * prod + both[:, :M])
        if not last:
            prod = 0.25 * (13.0 * prod - 15.0 * square + both[:, M:])
    w_ref[0], w_ref[1] = split_2(dot_wide(split_2(factor), split_2(approx)))


def reduce_kernel(parts_ref, out_ref):
    parts = parts_ref[...].astype(f32)
    level = (parts[:, 8] + parts[:, 9]) + parts[:, 10]
    weight = jnp.exp(level - jnp.max(level, axis=0, keepdims=True))
    weight = weight / jnp.sum(weight, axis=0, keepdims=True)
    out_ref[...] = jnp.sum(parts[:, 0:8] * weight[:, None, :], axis=0)


def middle_kernel(core_ref, own_ref, other_ref, w_ref, out_ref):
    own, other = own_ref[...], other_ref[...]
    is_first = core_ref[0] == 0
    bv = jnp.concatenate([jnp.where(is_first, own, other), jnp.where(is_first, other, own)], axis=1)
    mid = dot_wide(split_2(bv), (w_ref[0], w_ref[1]))
    rows = jnp.concatenate([mid[:, :128], mid[:, 128:]], axis=0)
    out_ref[...] = jnp.broadcast_to(rows.astype(bf16)[None], out_ref.shape)


def token_kernel(lk_ref, q_ref, out_ref):
    query = q_ref[...]
    lk = lk_ref[...].astype(f32)
    for head in range(HEADS):
        own = jnp.where(head_mask(head), lk, 0.0).astype(bf16)
        scores = dot_nt(own, query)
        expo = jnp.exp2((scores - jnp.max(scores, axis=0, keepdims=True)) * (SCALE * LOG2_E))
        out_ref[head] = (expo * (1.0 / jnp.sum(expo, axis=0, keepdims=True))).astype(bf16)


def conv_kernel(core_ref, vt_ref, near_ref, far_ref, cw_ref, out_ref):
    blocks = ROWS // 128
    is_first = core_ref[0] == 0
    near = near_ref[...].astype(f32)
    far = far_ref[...].astype(f32)
    empty = jnp.zeros((128 - HALF, WIDTH), f32)
    before = jnp.concatenate([empty, jnp.where(is_first, far, near)], axis=0).T.astype(bf16)
    after = jnp.concatenate([jnp.where(is_first, near, far), empty], axis=0).T.astype(bf16)
    for head in range(HEADS):
        taps = jnp.concatenate([cw_ref[head : head + 1, :], jnp.zeros((1, 384 - TAPS), f32)], axis=1)
        band = pltpu.roll(
            jnp.broadcast_to(taps, (128, 384)), 128 - HALF, 1, stride=1, stride_axis=0
        )
        high, low = split_2(band)
        rows = slice(head * HD, (head + 1) * HD)
        pieces = [before[rows, :]]
        pieces += [vt_ref[rows, b * 128 : b * 128 + 128] for b in range(blocks)]
        pieces += [after[rows, :]]
        windows = jnp.concatenate(
            [jnp.concatenate(pieces[b : b + 3] * 2, axis=1) for b in range(blocks)], axis=0
        )
        out = dot_nt(windows, jnp.concatenate([high, low], axis=1))
        for b in range(blocks):
            out_ref[rows, b * 128 : b * 128 + 128] = out[b * HD : (b + 1) * HD, :]


def attend_kernel(group_ref, mid_ref, kf_ref, conv_ref, *refs):
    out_refs, joined = refs[:-1], refs[-1]
    groups = len(out_refs)
    seg = ROWS // groups
    mid = mid_ref[...].astype(f32)
    mid = jnp.concatenate(
        [mid[:, :8].reshape(M, 128), mid[:, 8:].reshape(M, 128)], axis=1
    ).astype(bf16)
    outs = []
    for head in range(HEADS):
        rows = slice(head * HD, (head + 1) * HD)
        outs.append((dot_nn(mid[rows, :], kf_ref[head]) + conv_ref[rows, :]).astype(bf16))
    joined[...] = jnp.concatenate(outs, axis=0).T
    for step in range(groups):
        to = lax.rem(group_ref[0] + step, groups)
        out_refs[step][...] = joined[pl.ds(pl.multiple_of(to * seg, seg), seg), :]


def output_kernel(group_ref, w_ref, *refs):
    x_refs, (out_hbm, joined, out_ref, sems) = refs[:-4], refs[-4:]
    groups = len(x_refs)
    for step in range(groups):
        source = lax.rem(group_ref[0] + groups - step, groups)
        joined[:, pl.ds(pl.multiple_of(source * WIDTH, WIDTH), WIDTH)] = x_refs[step][...]
    copies = []
    for part in range(4):
        lanes = slice(part * 256, part * 256 + 256)
        out_ref[:, lanes] = dot_nn(joined[...], w_ref[:, lanes]).astype(bf16)
        copies.append(pltpu.make_async_copy(out_ref.at[:, lanes], out_hbm.at[:, lanes], sems.at[part]))
        copies[-1].start()
    for copy in copies:
        copy.wait()


def body(tokens, w_qkv, w_out, conv_weight):
    groups = lax.axis_size("head")
    same_core = [[2 * chip + core for chip in range(CHIPS)] for core in range(2)]
    swap = [(i, i ^ 1) for i in range(2 * CHIPS)]
    onward = [(2 * chip + 1, 2 * chip + 2) for chip in range(CHIPS - 1)]
    onward += [(b, a) for a, b in onward]
    place = lax.axis_index("ctx").astype(jnp.int32)
    group = lax.axis_index("head").astype(jnp.int32).reshape(1)
    seg = ROWS // groups
    core = (place % 2).reshape(1)
    head_id = (place // (2 * CHIPS // HEADS)).reshape(1)

    def exchange(x):
        return lax.all_to_all(x, "ctx", 0, 0, tiled=True, axis_index_groups=same_core)

    tokens_other = lax.ppermute(tokens, "ctx", swap)
    own = call(
        landmarks_kernel,
        shaped((CHIPS, 16, 128), bf16),
        [
            pltpu.VMEM((ROWS, 1024), bf16),
            pltpu.VMEM((2, 1024, WIDTH), bf16),
            pltpu.VMEM((16, 128), f32),
            pltpu.SemaphoreType.DMA((6,)),
        ],
        specs=[HBM, HBM],
        flops=2 * 16 * 1024 * 512,
        moved=3 * MIB,
        limit=63,
    )(tokens, w_qkv)
    land = exchange(own)
    key, value_t, key_other, value_other, near, far = call(
        project_kernel,
        [shaped((ROWS, WIDTH), bf16), shaped((WIDTH, ROWS), bf16)] * 2
        + [shaped((HALF, WIDTH), bf16)] * 2,
        [
            pltpu.VMEM((2, ROWS, 1024), bf16),
            pltpu.VMEM((2, 1024, WIDTH), bf16),
            pltpu.SemaphoreType.DMA((10,)),
        ],
        specs=[SMEM, HBM, HBM, HBM],
        limit=51,
        flops=4 * 1024 * 1024 * 512,
        moved=8 * MIB,
    )(core, tokens, tokens_other, w_qkv)
    land, key, value_t, near, far, key_other, value_other = lax.optimization_barrier(
        (land, key, value_t, near, far, key_other, value_other)
    )
    parts = call(
        scores_kernel,
        shaped((CHIPS, 16, 128), bf16),
        [pltpu.VMEM((CHIPS * 16, 128), f32)],
        n_in=5,
        flops=4 * 4 * 1024 * 256 * 256,
        moved=4 * MIB,
        exps=MIB,
    )(land, key, value_t, key_other, value_other)
    gathered = exchange(parts)
    land, parts = lax.optimization_barrier((land, parts))
    land_other = lax.ppermute(land, "ctx", swap)
    land_k, inverse = call(
        pinv_kernel,
        [shaped((M, WIDTH), bf16), shaped((2, M, M), bf16)],
        [pltpu.VMEM((CHIPS * 32, 128), f32)],
        specs=[SMEM, SMEM, VMEM, VMEM],
        flops=24 * 3 * 2 * 256**3,
        moved=MIB // 2,
        exps=65536,
    )(core, head_id, land, land_other)
    gathered, inverse = lax.optimization_barrier((gathered, inverse))
    reduced = call(
        reduce_kernel, shaped((8, 128), f32), flops=32 * 8 * 128 * 2, moved=MIB // 8
    )(gathered)
    reduced_other = lax.ppermute(reduced, "ctx", swap)
    mid_own = call(
        middle_kernel,
        shaped((CHIPS, 16, 128), bf16),
        specs=[SMEM] + [VMEM] * 3,
        flops=6 * 8 * 256 * 256,
        moved=MIB // 2,
    )(core, reduced, reduced_other, inverse)
    late_tokens, late_w, mid_own = lax.optimization_barrier((tokens, w_qkv, mid_own))
    query = call(
        query_kernel,
        shaped((ROWS, WIDTH), bf16),
        n_in=2,
        flops=2 * 1024 * 1024 * 256,
        moved=4 * MIB,
    )(late_tokens, late_w)
    mids = exchange(mid_own)
    far = lax.ppermute(far, "ctx", onward)
    kernel_f = call(
        token_kernel,
        shaped((HEADS, M, ROWS), bf16),
        n_in=2,
        flops=4 * 2 * 1024 * 256 * 256,
        moved=3 * MIB,
        exps=MIB,
    )(land_k, query)
    far, kernel_f = lax.optimization_barrier((far, kernel_f))
    conv = call(
        conv_kernel,
        shaped((WIDTH, ROWS), f32),
        specs=[SMEM] + [VMEM] * 4,
        flops=2 * 512 * 768 * 512,
        moved=2 * MIB,
    )(core, value_t, near, far, conv_weight)
    mids, kernel_f, conv = lax.optimization_barrier((mids, kernel_f, conv))
    head_out = call(
        attend_kernel,
        [shaped((seg, WIDTH), bf16)] * groups,
        [pltpu.VMEM((ROWS, WIDTH), bf16)],
        specs=[SMEM] + [VMEM] * 3,
        flops=4 * 2 * 64 * 256 * 1024,
        moved=4 * MIB,
    )(group, mids, kernel_f, conv)
    arrived = [head_out[0]]
    for step in range(1, groups):
        ring = [(i, (i + step) % groups) for i in range(groups)]
        arrived.append(lax.ppermute(head_out[step], "head", ring))
    return call(
        output_kernel,
        shaped((seg, w_out.shape[1]), bf16),
        [
            pltpu.VMEM((seg, w_out.shape[0]), bf16),
            pltpu.VMEM((seg, w_out.shape[1]), bf16),
            pltpu.SemaphoreType.DMA((4,)),
        ],
        specs=[SMEM] + [VMEM] * (1 + groups),
        out_specs=HBM,
        flops=2 * 256 * 1024 * 1024,
        moved=3 * MIB,
    )(group, w_out, *arrived)


def solution(mesh):
    placed = (P("ctx", None), P(None, None, "head"), P(), P("head", None))
    return jax.shard_map(
        body, mesh=mesh, in_specs=placed, out_specs=P(("ctx", "head"), None), check_vma=False
    )
```

```python
import jax
import jax.numpy as jnp
from jax import lax
from jax.experimental import pallas as pl
from jax.experimental.pallas import tpu as pltpu
from jax.sharding import PartitionSpec as P

M = 256
NS_STEPS = 6
TAPS = 33
HALF = 16
HEADS = 4
HD = 64
WIDTH = 256
CHIPS = 32
ROWS = 1024
SCALE = 0.125
LOG2_E = 1.4426950408889634
f32 = jnp.float32
bf16 = jnp.bfloat16
INTERPRET = False
VMEM = pl.BlockSpec(memory_space=pltpu.VMEM)
SMEM = pl.BlockSpec(memory_space=pltpu.SMEM)
HBM = pl.BlockSpec(memory_space=pltpu.HBM)
MIB = 1 << 20


def call(
    kernel, outs, scratch=(), specs=None, out_specs=None, n_in=1, flops=0, moved=0, exps=0, limit=24
):
    single = not isinstance(outs, (list, tuple))
    return pl.pallas_call(
        kernel,
        out_shape=outs,
        in_specs=specs or [VMEM] * n_in,
        out_specs=out_specs or (VMEM if single else [VMEM] * len(outs)),
        scratch_shapes=list(scratch),
        compiler_params=pltpu.CompilerParams(vmem_limit_bytes=limit * MIB),
        cost_estimate=pl.CostEstimate(flops=flops, bytes_accessed=moved, transcendentals=exps),
        interpret=INTERPRET,
    )


def shaped(shape, dtype):
    return jax.ShapeDtypeStruct(shape, dtype)


def dot_nn(a, b):
    return lax.dot_general(a, b, (((1,), (0,)), ((), ())), preferred_element_type=f32)


def dot_nt(a, b):
    return lax.dot_general(a, b, (((1,), (1,)), ((), ())), preferred_element_type=f32)


def split_2(x):
    high = x.astype(bf16)
    return high, (x - high.astype(f32)).astype(bf16)


def split_3(x):
    high = x.astype(bf16)
    rest = x - high.astype(f32)
    middle = rest.astype(bf16)
    return high, middle, (rest - middle.astype(f32)).astype(bf16)


def dot_wide(a, b, transposed=False):
    (ah, al), (bh, bl) = a, b
    left = jnp.concatenate([ah, ah, al], axis=1)
    if transposed:
        return dot_nt(left, jnp.concatenate([bh, bl, bh], axis=1))
    return dot_nn(left, jnp.concatenate([bh, bl, bh], axis=0))


def head_mask(head):
    lane = lax.broadcasted_iota(jnp.int32, (M, WIDTH), 1)
    return (lane >= head * HD) & (lane < (head + 1) * HD)


def landmarks_kernel(tok_hbm, w_hbm, out_ref, tok_ref, w_ref, rows_ref, sems):
    seg = ROWS // 4
    copies = [
        pltpu.make_async_copy(
            tok_hbm.at[s * seg : (s + 1) * seg, :], tok_ref.at[s * seg : (s + 1) * seg, :], sems.at[s]
        )
        for s in range(4)
    ] + [pltpu.make_async_copy(w_hbm.at[c], w_ref.at[c], sems.at[4 + c]) for c in range(2)]
    for copy in copies:
        copy.start()
    sums = []
    for s in range(4):
        copies[s].wait()
        sums.append(
            jnp.sum(tok_ref[s * seg : (s + 1) * seg, :].astype(f32), axis=0, keepdims=True)
        )
    means = jnp.concatenate(sums, axis=0) * (1.0 / seg)
    high, low = split_2(means)
    stacked = jnp.concatenate([high.astype(f32), low.astype(f32)], axis=0).astype(bf16)
    for kind in range(2):
        copies[4 + kind].wait()
        product = dot_nn(stacked, w_ref[kind])
        land = product[0:4] + product[4:8]
        for half in range(2):
            rows_ref[pl.ds(2 * kind + half, 4, stride=4), :] = land[:, half * 128 : half * 128 + 128]
    out_ref[...] = jnp.broadcast_to(rows_ref[...].astype(bf16)[None], out_ref.shape)


def project_kernel(
    core_ref,
    own_hbm,
    other_hbm,
    w_hbm,
    k_ref,
    vt_ref,
    k2_ref,
    vt2_ref,
    near_ref,
    far_ref,
    tok_ref,
    w_ref,
    sems,
):
    cut = ROWS // 4
    loads = [pltpu.make_async_copy(w_hbm.at[1 + c], w_ref.at[c], sems.at[8 + c]) for c in range(2)]
    copies = [
        pltpu.make_async_copy(
            source.at[s * cut : (s + 1) * cut, :],
            tok_ref.at[side, s * cut : (s + 1) * cut, :],
            sems.at[4 * side + s],
        )
        for side, source in enumerate((own_hbm, other_hbm))
        for s in range(4)
    ]
    for copy in loads + copies:
        copy.start()
    for copy in loads:
        copy.wait()
    edges = []
    for side, (key_ref, value_ref) in enumerate(((k_ref, vt_ref), (k2_ref, vt2_ref))):
        for s in range(4):
            copies[4 * side + s].wait()
            rows = slice(s * cut, (s + 1) * cut)
            tok = tok_ref[side, rows, :]
            key_ref[rows, :] = dot_nn(tok, w_ref[0]).astype(bf16)
            value = dot_nn(tok, w_ref[1]).astype(bf16)
            value_ref[:, rows] = value.T
            edges.append(value)
    is_first = core_ref[0] == 0
    first, last = edges[0][:HALF].astype(f32), edges[3][cut - HALF :].astype(f32)
    far_ref[...] = jnp.where(is_first, first, last).astype(bf16)
    first, last = edges[4][:HALF].astype(f32), edges[7][cut - HALF :].astype(f32)
    near_ref[...] = jnp.where(is_first, first, last).astype(bf16)


def query_kernel(tok_ref, w_ref, q_ref):
    q_ref[...] = dot_nn(tok_ref[...], w_ref[0]).astype(bf16)


def pick_rows(land_rows, first, count, at):
    return jnp.concatenate(
        [land_rows[pl.ds(first + at + half, count, stride=4), :] for half in range(2)], axis=1
    )


def scores_kernel(land_ref, k_ref, vt_ref, k2_ref, vt2_ref, out_ref, land_rows):
    land_rows[...] = land_ref[...].astype(f32).reshape(CHIPS * 16, 128)
    lq = pick_rows(land_rows, 0, CHIPS * 4, 0)
    lane = lax.broadcasted_iota(jnp.int32, lq.shape, 1)
    own = [
        jnp.concatenate(
            [
                jnp.where((lane >= head * HD) & (lane < (head + 1) * HD), lq, 0.0)
                for head in (2 * pair, 2 * pair + 1)
            ],
            axis=0,
        ).astype(bf16)
        for pair in range(2)
    ]
    found = []
    keys, values = (k_ref, k2_ref), (vt_ref, vt2_ref)
    ahead = dot_nt(keys[0][...], own[0])
    for step in range(4):
        side, pair = step // 2, step % 2
        scores = ahead
        if step < 3:
            ahead = dot_nt(keys[(step + 1) // 2][...], own[1 - pair])
        top = jnp.max(scores, axis=0, keepdims=True)
        expo = jnp.exp2((scores - top) * (SCALE * LOG2_E))
        total = jnp.sum(expo, axis=0, keepdims=True)
        rows = slice(pair * 128, pair * 128 + 128)
        found.append((top, total, dot_nn(values[side][rows, :], expo.astype(bf16))))
    each = CHIPS // HEADS
    for pair in range(2):
        top_a, total_a, sum_a = found[pair]
        top_b, total_b, sum_b = found[2 + pair]
        top = jnp.maximum(top_a, top_b)
        scale_a = jnp.exp((top_a - top) * SCALE)
        scale_b = jnp.exp((top_b - top) * SCALE)
        total = total_a * scale_a + total_b * scale_b
        mean = sum_a * (scale_a / total) + sum_b * (scale_b / total)
        level = [p.astype(f32) for p in split_3(top * SCALE + jnp.log(total))]
        level = jnp.concatenate(level + [jnp.zeros((5, 256), f32)], axis=0)
        for side in range(2):
            lanes = slice(side * 128, side * 128 + 128)
            block = mean[side * HD : (side + 1) * HD, lanes].reshape(each, 8, 128)
            tail = jnp.broadcast_to(level[None, :, lanes], (each, 8, 128))
            at = (2 * pair + side) * each
            out_ref[at : at + each] = jnp.concatenate([block, tail], axis=1).astype(bf16)


def pinv_kernel(core_ref, head_ref, own_ref, other_ref, lk_ref, w_ref, land_rows):
    core = core_ref[0]
    count = CHIPS * 16
    land_rows[pl.ds(core * count, count), :] = own_ref[...].astype(f32).reshape(count, 128)
    land_rows[pl.ds((1 - core) * count, count), :] = other_ref[...].astype(f32).reshape(count, 128)
    lk_ref[...] = pick_rows(land_rows, 0, M, 2).astype(bf16)
    own = jnp.where(head_mask(head_ref[0]), pick_rows(land_rows, 0, M, 0), 0.0).astype(bf16)
    scores = dot_nt(own, lk_ref[...]) * SCALE
    expo = jnp.exp(scores - jnp.max(scores, axis=1, keepdims=True))
    kernel = expo / jnp.sum(expo, axis=1, keepdims=True)
    col_sum = jnp.max(jnp.sum(kernel, axis=0, keepdims=True))
    row_sum = jnp.max(jnp.sum(kernel, axis=1, keepdims=True))
    approx = kernel / (col_sum * row_sum)
    diagonal = lax.broadcasted_iota(jnp.int32, (M, M), 0) == lax.broadcasted_iota(jnp.int32, (M, M), 1)
    ident = jnp.where(diagonal, 1.0, 0.0)
    prod = dot_wide(split_2(approx), split_2(kernel), transposed=True)
    factor = None
    for step in range(NS_STEPS):
        parts = split_2(prod)
        square = dot_wide(parts, parts)
        if factor is not None:
            approx = dot_wide(split_2(factor), split_2(approx))
        last = step == NS_STEPS - 1
        right = 7.0 * ident - prod
        if not last:
            right = jnp.concatenate([right, 7.0 * prod - square], axis=1)
        both = dot_wide(split_2(square), split_2(right))
        factor = 0.25 * (13.0 * ident - 15.0 * prod + both[:, :M])
        if not last:
            prod = 0.25 * (13.0 * prod - 15.0 * square + both[:, M:])
    w_ref[0], w_ref[1] = split_2(dot_wide(split_2(factor), split_2(approx)))


def reduce_kernel(parts_ref, out_ref):
    parts = parts_ref[...].astype(f32)
    level = (parts[:, 8] + parts[:, 9]) + parts[:, 10]
    weight = jnp.exp(level - jnp.max(level, axis=0, keepdims=True))
    total = jnp.sum(weight, axis=0, keepdims=True)
    out_ref[...] = jnp.sum(parts[:, 0:8] * weight[:, None, :], axis=0) / total


def middle_kernel(core_ref, own_ref, other_ref, w_ref, out_ref):
    own, other = own_ref[...], other_ref[...]
    is_first = core_ref[0] == 0
    bv = jnp.concatenate([jnp.where(is_first, own, other), jnp.where(is_first, other, own)], axis=1)
    mid = dot_wide(split_2(bv), (w_ref[0], w_ref[1]))
    rows = jnp.concatenate([mid[:, :128], mid[:, 128:]], axis=0)
    out_ref[...] = jnp.broadcast_to(rows.astype(bf16)[None], out_ref.shape)


def token_kernel(lk_ref, q_ref, out_ref):
    query = q_ref[...]
    lk = lk_ref[...].astype(f32)
    for head in range(HEADS):
        own = jnp.where(head_mask(head), lk, 0.0).astype(bf16)
        scores = dot_nt(own, query)
        expo = jnp.exp2((scores - jnp.max(scores, axis=0, keepdims=True)) * (SCALE * LOG2_E))
        out_ref[head] = (expo * (1.0 / jnp.sum(expo, axis=0, keepdims=True))).astype(bf16)


def conv_kernel(core_ref, vt_ref, near_ref, far_ref, cw_ref, out_ref):
    blocks = ROWS // 128
    is_first = core_ref[0] == 0
    near = near_ref[...].astype(f32)
    far = far_ref[...].astype(f32)
    empty = jnp.zeros((128 - HALF, WIDTH), f32)
    before = jnp.concatenate([empty, jnp.where(is_first, far, near)], axis=0).T.astype(bf16)
    after = jnp.concatenate([jnp.where(is_first, near, far), empty], axis=0).T.astype(bf16)
    for head in range(HEADS):
        taps = jnp.concatenate([cw_ref[head : head + 1, :], jnp.zeros((1, 384 - TAPS), f32)], axis=1)
        band = pltpu.roll(
            jnp.broadcast_to(taps, (128, 384)), 128 - HALF, 1, stride=1, stride_axis=0
        )
        high, low = split_2(band)
        rows = slice(head * HD, (head + 1) * HD)
        pieces = [before[rows, :]]
        pieces += [vt_ref[rows, b * 128 : b * 128 + 128] for b in range(blocks)]
        pieces += [after[rows, :]]
        windows = jnp.concatenate(
            [jnp.concatenate(pieces[b : b + 3] * 2, axis=1) for b in range(blocks)], axis=0
        )
        out = dot_nt(windows, jnp.concatenate([high, low], axis=1))
        for b in range(blocks):
            out_ref[rows, b * 128 : b * 128 + 128] = out[b * HD : (b + 1) * HD, :]


def attend_kernel(group_ref, mid_ref, kf_ref, conv_ref, *refs):
    out_refs, joined = refs[:-1], refs[-1]
    groups = len(out_refs)
    seg = ROWS // groups
    mid = mid_ref[...].astype(f32)
    mid = jnp.concatenate(
        [mid[:, :8].reshape(M, 128), mid[:, 8:].reshape(M, 128)], axis=1
    ).astype(bf16)
    outs = []
    for head in range(HEADS):
        rows = slice(head * HD, (head + 1) * HD)
        outs.append((dot_nn(mid[rows, :], kf_ref[head]) + conv_ref[rows, :]).astype(bf16))
    joined[...] = jnp.concatenate(outs, axis=0).T
    for step in range(groups):
        to = lax.rem(group_ref[0] + step, groups)
        out_refs[step][...] = joined[pl.ds(pl.multiple_of(to * seg, seg), seg), :]


def output_kernel(group_ref, w_ref, *refs):
    x_refs, (out_hbm, joined, out_ref, sems) = refs[:-4], refs[-4:]
    groups = len(x_refs)
    for step in range(groups):
        source = lax.rem(group_ref[0] + groups - step, groups)
        joined[:, pl.ds(pl.multiple_of(source * WIDTH, WIDTH), WIDTH)] = x_refs[step][...]
    copies = []
    for part in range(4):
        lanes = slice(part * 256, part * 256 + 256)
        out_ref[:, lanes] = dot_nn(joined[...], w_ref[:, lanes]).astype(bf16)
        copies.append(pltpu.make_async_copy(out_ref.at[:, lanes], out_hbm.at[:, lanes], sems.at[part]))
        copies[-1].start()
    for copy in copies:
        copy.wait()


def body(tokens, w_qkv, w_out, conv_weight):
    groups = lax.axis_size("head")
    same_core = [[2 * chip + core for chip in range(CHIPS)] for core in range(2)]
    swap = [(i, i ^ 1) for i in range(2 * CHIPS)]
    onward = [(2 * chip + 1, 2 * chip + 2) for chip in range(CHIPS - 1)]
    onward += [(b, a) for a, b in onward]
    place = lax.axis_index("ctx").astype(jnp.int32)
    group = lax.axis_index("head").astype(jnp.int32).reshape(1)
    seg = ROWS // groups
    core = (place % 2).reshape(1)
    head_id = (place // (2 * CHIPS // HEADS)).reshape(1)

    def exchange(x):
        return lax.all_to_all(x, "ctx", 0, 0, tiled=True, axis_index_groups=same_core)

    tokens_other = lax.ppermute(tokens, "ctx", swap)
    own = call(
        landmarks_kernel,
        shaped((CHIPS, 16, 128), bf16),
        [
            pltpu.VMEM((ROWS, 1024), bf16),
            pltpu.VMEM((2, 1024, WIDTH), bf16),
            pltpu.VMEM((16, 128), f32),
            pltpu.SemaphoreType.DMA((6,)),
        ],
        specs=[HBM, HBM],
        flops=2 * 16 * 1024 * 512,
        moved=3 * MIB,
        limit=63,
    )(tokens, w_qkv)
    land = exchange(own)
    key, value_t, key_other, value_other, near, far = call(
        project_kernel,
        [shaped((ROWS, WIDTH), bf16), shaped((WIDTH, ROWS), bf16)] * 2
        + [shaped((HALF, WIDTH), bf16)] * 2,
        [
            pltpu.VMEM((2, ROWS, 1024), bf16),
            pltpu.VMEM((2, 1024, WIDTH), bf16),
            pltpu.SemaphoreType.DMA((10,)),
        ],
        specs=[SMEM, HBM, HBM, HBM],
        limit=51,
        flops=4 * 1024 * 1024 * 512,
        moved=8 * MIB,
    )(core, tokens, tokens_other, w_qkv)
    land, key, value_t, near, far, key_other, value_other = lax.optimization_barrier(
        (land, key, value_t, near, far, key_other, value_other)
    )
    parts = call(
        scores_kernel,
        shaped((CHIPS, 16, 128), bf16),
        [pltpu.VMEM((CHIPS * 16, 128), f32)],
        n_in=5,
        flops=4 * 4 * 1024 * 256 * 256,
        moved=4 * MIB,
        exps=MIB,
    )(land, key, value_t, key_other, value_other)
    gathered = exchange(parts)
    land, parts = lax.optimization_barrier((land, parts))
    land_other = lax.ppermute(land, "ctx", swap)
    land_k, inverse = call(
        pinv_kernel,
        [shaped((M, WIDTH), bf16), shaped((2, M, M), bf16)],
        [pltpu.VMEM((CHIPS * 32, 128), f32)],
        specs=[SMEM, SMEM, VMEM, VMEM],
        flops=24 * 3 * 2 * 256**3,
        moved=MIB // 2,
        exps=65536,
    )(core, head_id, land, land_other)
    gathered, inverse = lax.optimization_barrier((gathered, inverse))
    reduced = call(
        reduce_kernel, shaped((8, 128), f32), flops=32 * 8 * 128 * 2, moved=MIB // 8
    )(gathered)
    reduced_other = lax.ppermute(reduced, "ctx", swap)
    mid_own = call(
        middle_kernel,
        shaped((CHIPS, 16, 128), bf16),
        specs=[SMEM] + [VMEM] * 3,
        flops=6 * 8 * 256 * 256,
        moved=MIB // 2,
    )(core, reduced, reduced_other, inverse)
    late_tokens, late_w, mid_own = lax.optimization_barrier((tokens, w_qkv, mid_own))
    query = call(
        query_kernel,
        shaped((ROWS, WIDTH), bf16),
        n_in=2,
        flops=2 * 1024 * 1024 * 256,
        moved=4 * MIB,
    )(late_tokens, late_w)
    mids = exchange(mid_own)
    far = lax.ppermute(far, "ctx", onward)
    kernel_f = call(
        token_kernel,
        shaped((HEADS, M, ROWS), bf16),
        n_in=2,
        flops=4 * 2 * 1024 * 256 * 256,
        moved=3 * MIB,
        exps=MIB,
    )(land_k, query)
    far, kernel_f = lax.optimization_barrier((far, kernel_f))
    conv = call(
        conv_kernel,
        shaped((WIDTH, ROWS), f32),
        specs=[SMEM] + [VMEM] * 4,
        flops=2 * 512 * 768 * 512,
        moved=2 * MIB,
    )(core, value_t, near, far, conv_weight)
    mids, kernel_f, conv = lax.optimization_barrier((mids, kernel_f, conv))
    head_out = call(
        attend_kernel,
        [shaped((seg, WIDTH), bf16)] * groups,
        [pltpu.VMEM((ROWS, WIDTH), bf16)],
        specs=[SMEM] + [VMEM] * 3,
        flops=4 * 2 * 64 * 256 * 1024,
        moved=4 * MIB,
    )(group, mids, kernel_f, conv)
    arrived = [head_out[0]]
    for step in range(1, groups):
        ring = [(i, (i + step) % groups) for i in range(groups)]
        arrived.append(lax.ppermute(head_out[step], "head", ring))
    return call(
        output_kernel,
        shaped((seg, w_out.shape[1]), bf16),
        [
            pltpu.VMEM((seg, w_out.shape[0]), bf16),
            pltpu.VMEM((seg, w_out.shape[1]), bf16),
            pltpu.SemaphoreType.DMA((4,)),
        ],
        specs=[SMEM] + [VMEM] * (1 + groups),
        out_specs=HBM,
        flops=2 * 256 * 1024 * 1024,
        moved=3 * MIB,
    )(group, w_out, *arrived)


def solution(mesh):
    placed = (P("ctx", None), P(None, None, "head"), P(), P("head", None))
    return jax.shard_map(
        body, mesh=mesh, in_specs=placed, out_specs=P(("ctx", "head"), None), check_vma=False
    )
```
